128 devices in a mesh: row: 8 (over z, core), col: 16 (over x, y).
Axes of the slice: x: 4, y: 4, z: 4, core: 2. Of those that a mesh axis runs over, the one named last changes fastest.
Arguments:
- gradient: bfloat16 [8192, 8192], P('row', 'col'), may hold values from -1.5 to 1.5
- stat_old: float32 [8192, 8192], P('row', 'col'), may hold values from -6 to 6
- inv_root: bfloat16 [8192, 8192], P('row'), may hold values from -0.0625 to 0.0625
Outputs:
- stat_new: float32 [8192, 8192], P('row', 'col')
- preconditioned: bfloat16 [8192, 8192], P('row', 'col')
The draws below stay inside these ranges and needn't reach their ends.
All inputs are finite; a program needn't handle non-finite values.
Results may differ from the reference program's by a relative error of at most 0.012.
Values may be sent and summed in bfloat16 or wider, within the bound.
No kernel may reach another device: no remote copies, remote signals or barrier semaphores. Data moves between devices by JAX's collectives and lax.ppermute only.
A program may use at most 192 MiB of HBM per device.

```python
import jax
import jax.numpy as jnp
from jax import lax

D = 8192
LAT = 8192


def levels(own_key, dims, pieces, least, largest):
    factor_of, own = 1.0, jax.random.fold_in(own_key, 6)
    for dim, blocks in pieces:
        draws = jnp.exp(jax.random.uniform(jax.random.fold_in(own, dim), (blocks,), jnp.float32, least / len(pieces), largest / len(pieces)))
        factor_of = factor_of * jnp.repeat(draws, dims[dim] // blocks).reshape([-1 if axis == dim else 1 for axis in range(len(dims))])
    return factor_of


def gaussian(rng, dims, scale, bound, cuts=(), held_as=jnp.bfloat16):
    entries = jax.random.normal(rng, dims, jnp.float32) * scale
    if len(cuts) > 0:
        entries = levels(rng, dims, cuts, -0.22, 0.18) * entries
    return jnp.clip(entries, min=-bound, max=bound).astype(held_as)


def setup_inputs(seed: int = 0) -> dict:
    arg_keys = jax.random.split(jax.random.key(seed), 4)
    return {
        "gradient": gaussian(arg_keys[0], (D, LAT), 0.25, 1.5, ((0, 8), (1, 16))),
        "stat_old": gaussian(arg_keys[1], (D, D), 1.0, 6.0, ((0, 8), (1, 16)), jnp.float32),
        "inv_root": gaussian(arg_keys[2], (D, D), D ** -0.5, 0.0625, ((0, 8),)),
    }


def reference(gradient, stat_old, inv_root):
    wide = gradient.astype(jnp.float32)
    gram = jnp.dot(wide, wide.T, precision=lax.Precision.HIGHEST, preferred_element_type=jnp.float32)
    stat_new = 0.9 * stat_old + 0.1 * gram
    product = jnp.dot(inv_root.astype(jnp.float32), wide, precision=lax.Precision.HIGHEST, preferred_element_type=jnp.float32)
    return stat_new, product.astype(jnp.bfloat16)
```

```python
import functools

import jax
import jax.numpy as jnp
import numpy as np
from jax import lax
from jax.sharding import Mesh
from jax.sharding import PartitionSpec as P

N = 4
AXES = ("z", "core", "x", "y")
F32 = jnp.float32
BF16 = jnp.bfloat16


def linear(z, k, x, y):
    return (((z % N) * 2 + k) * N + x % N) * N + y % N


def devices():
    return [(z, k, x, y) for z in range(N) for k in range(2) for x in range(N) for y in range(N)]


def send(value, where):
    pairs = []
    for device in devices():
        to = where(*device)
        if to is not None:
            pairs.append((linear(*device), linear(*to)))
    return lax.ppermute(value, AXES, pairs)


def sign(k):
    return 1 - 2 * k


def along(axis, steps):
    def where(z, k, x, y):
        n = steps(k)
        return {"x": (z, k, x + n, y), "y": (z, k, x, y + n), "z": (z + n, k, x, y)}[axis]

    return where


def other_core(value):
    return send(value, lambda z, k, x, y: (z, 1 - k, x, y))


def add(*terms):
    total = terms[0].astype(F32)
    for term in terms[1:]:
        total = total + term.astype(F32)
    return total.astype(BF16)


def reduce_ring(parts, axis):
    total = parts[0]
    for part in parts[1:]:
        total = add(send(total, along(axis, sign)), part)
    return total


def reduce_direct(parts, axis):
    got = [send(parts[r], along(axis, lambda k, r=r: -sign(k) * (1 + r))) for r in range(N - 1)]
    return add(*got, parts[N - 1])


def pick(stacked, index):
    return lax.dynamic_index_in_dim(stacked, index, 0, keepdims=False)


@functools.cache
def final_plan():
    edges = []
    for z, k, x, y in devices():
        p = (y + (1 if x < z else 0) + k) % N
        edges.append(((z, k, x, y), (z, p // 2, x, y), p % 2, 0))
        if not (x == z and k == 0):
            edges.append(((z, k, x, y), (x, y // 2, z, p), y % 2, 1))
    touching = {}
    for n, (source, target, _, _) in enumerate(edges):
        touching.setdefault(("from", source), []).append(n)
        touching.setdefault(("to", target), []).append(n)
    colour = {}
    for first in sorted(range(len(edges)), key=lambda n: min(len(touching[("from", edges[n][0])]), len(touching[("to", edges[n][1])]))):
        stack = [(first, 0)]
        while stack:
            n, c = stack.pop()
            if n in colour:
                assert colour[n] == c or n == first
                continue
            colour[n] = c
            for end in (("from", edges[n][0]), ("to", edges[n][1])):
                assert len(touching[end]) <= 2
                stack.extend((m, 1 - c) for m in touching[end] if m != n)
    routes = [{}, {}]
    view = np.full((2 * N**3, 2), 4, np.int32)
    for n, (source, target, slot, turned) in enumerate(edges):
        assert source not in routes[colour[n]] and view[linear(*target), slot] == 4
        routes[colour[n]][source] = target
        view[linear(*target), slot] = 2 * colour[n] + turned
    return routes, view


def on_device(gradient, stat_old, inv_root):
    rows, lat = gradient.shape
    H = rows // 2
    Q = H // N
    z, k, x, y = (lax.axis_index(name) for name in AXES)
    s = 1 - 2 * k

    tiles = [gradient]
    for _ in range(N - 1):
        tiles.append(send(tiles[-1], along("z", sign)))
    whole = []
    for tile in tiles:
        both = jnp.stack([tile, other_core(tile)])
        whole.append(jnp.stack([pick(both, k), pick(both, 1 - k)]))

    behind_x = [(x - s * (1 + r)) % N for r in range(N)]
    behind_y = [(y - s * (1 + r)) % N for r in range(N)]
    own = whole[0].reshape(N, N, Q, lat)
    own = jnp.stack([lax.dynamic_index_in_dim(own, c, 1, keepdims=False) for c in behind_x], 1)
    extra = lax.dynamic_index_in_dim(whole[0].reshape(N, 2, N, Q // 2, lat), k, 1, keepdims=False)
    extra = jnp.stack([lax.dynamic_index_in_dim(extra, c, 1, keepdims=False) for c in behind_x], 1)

    def plane(b, q):
        return jnp.where(q < 2, (z - b) % N, (z + b) % N)

    reduced = []
    product = None
    root = inv_root.reshape(inv_root.shape[0], 2 * N, rows)
    for b in range(N):
        blocks = whole[b].reshape(N, H, lat)
        left, right = [], []
        for q in behind_y:
            p = (q + jnp.where(plane(b, q) < z, 1, 0) + k) % N
            a = pick(own, p)
            if b == 0:
                a = jnp.concatenate([a, pick(extra, (q + 2) % N)], 1)
            left.append(a.reshape(-1, lat))
            right.append(pick(blocks, q))
        share = jnp.einsum("qal,qbl->qab", jnp.stack(left), jnp.stack(right), preferred_element_type=F32).astype(BF16)
        share = share.reshape(N, N, -1, H)
        reduce = reduce_direct if b == N - 1 else reduce_ring
        first, second = share[..., : H // 2], share[..., H // 2 :]
        first = reduce([first[:, r] for r in range(N)], "x")
        second = reduce([second[r] for r in range(N)], "y")
        first = reduce([first[r] for r in range(N)], "y")
        second = reduce([second[r] for r in range(N)], "x")
        reduced.append(jnp.concatenate([first, second], 1))
        for half, turn in enumerate((-b, b)):
            columns = lax.dynamic_index_in_dim(root, 2 * ((z + turn) % N) + half, 1, keepdims=False)
            term = jnp.dot(columns, whole[b][half], preferred_element_type=F32)
            product = term if product is None else product + term

    diagonal = reduced[0][Q:]
    quarters = jnp.stack([reduced[0][:Q], *reduced[1:]])
    got, got_diagonal = [], []
    for d in range(N):
        to = (x + d) % N
        piece = pick(quarters, jnp.where(y < 2, z - to, to - z) % N)
        if d > 0:
            piece = send(piece, along("x", lambda k, d=d: d))
            diagonal_piece = send(diagonal, lambda z, k, x, y, d=d: (z, k, x + d, y) if (x + d) % N == z else None)
        else:
            diagonal_piece = diagonal
        got.append(piece)
        got_diagonal.append(diagonal_piece)
    got, got_diagonal = jnp.stack(got), jnp.stack(got_diagonal)
    block = jnp.concatenate([pick(got, (x - c) % N) for c in range(N)], 0)
    half = jnp.concatenate([pick(got_diagonal, (x - c) % N) for c in range(N)], 0)

    routes, view = final_plan()
    arrived = [send(block, lambda *device, route=route: route.get(device)) for route in routes]
    other_half = send(half, lambda z, k, x, y: (z, 1 - k, x, y) if x == z and k != ((y + 2) % N) // 2 else None)
    diagonal_block = jnp.where(k == 0, jnp.concatenate([half, other_half]), jnp.concatenate([other_half, half]))
    here = jnp.asarray(view)[((z * 2 + k) * N + x) * N + y]
    stat = []
    for slot in range(2):
        which = here[slot]
        value = jnp.where(which < 2, arrived[0], arrived[1])
        value = jnp.where(which % 2 == 1, value.T, value)
        value = jnp.where(which == 4, diagonal_block, value)
        stat.append(0.9 * stat_old[slot * H : (slot + 1) * H] + 0.1 * value.astype(F32))
    return jnp.concatenate(stat), product.astype(BF16)


def solution(mesh):
    fine = Mesh(mesh.devices.reshape(N, 2, N, N), AXES)
    row, col = ("z", "core"), ("x", "y")
    return jax.shard_map(
        on_device,
        mesh=fine,
        in_specs=(P(row, col), P(row, col), P(row, None)),
        out_specs=(P(row, col), P(row, col)),
        check_vma=False,
    )
```

```python
import functools

import jax
import jax.numpy as jnp
import numpy as np
from jax import lax
from jax.experimental import pallas as pl
from jax.experimental.pallas import tpu as pltpu
from jax.sharding import Mesh
from jax.sharding import PartitionSpec as P

N = 4
AXES = ("z", "core", "x", "y")
OFFSETS = (1, 3, 2, 0)
F32 = jnp.float32
BF16 = jnp.bfloat16


def linear(z, k, x, y):
    return (((z % N) * 2 + k) * N + x % N) * N + y % N


def devices():
    return [(z, k, x, y) for z in range(N) for k in range(2) for x in range(N) for y in range(N)]


def send(value, where):
    return lax.ppermute(value, AXES, [(linear(*device), linear(*where(*device))) for device in devices()])


def up(n):
    return lambda z, k, x, y: (z + n, k, x, y)


def other_core(value):
    return send(value, lambda z, k, x, y: (z, 1 - k, x, y))


def block_row(z, k, j, q):
    return (q + jnp.where(j < z, 1, 0) + (k + jnp.where(q >= 2, 1, 0)) % 2) % N


def place(distance):
    return jnp.where(distance == 1, 0, jnp.where(distance == 3, 1, jnp.where(distance == 2, 2, 3)))


def shares(mine, theirs, others, turns, diagonal):
    rows, lat = mine.shape
    H = rows // 2
    Q = H // N
    E = Q // 2 if diagonal else 0
    n = len(turns)
    tall = Q + E

    def kernel(mine_ref, theirs_ref, *refs):
        out_ref = refs[-1]
        z, k, x, y = (lax.axis_index(name) for name in AXES)

        def rows_of(block, part, parts):
            start = pl.multiple_of((block % 2) * H + part * (H // parts), H // parts)
            window = pl.ds(start, H // parts)
            return jnp.where(block // 2 == k, mine_ref[window, :], theirs_ref[window, :])

        for t, turn in enumerate(turns):
            j = (z + turn) % N
            for i in range(N):
                q = 2 * (k if i < 2 else 1 - k) + i % 2
                p = block_row(z, k, j, q)
                right = (refs[2 * t + i // 2])[(i % 2) * H : (i % 2 + 1) * H, :]
                left = []
                for offset in OFFSETS:
                    c = (x + offset) % N
                    left.append(rows_of(p, c, N))
                    if diagonal:
                        left.append(rows_of((q + 2) % N, k * N + c, 2 * N))
                result = lax.dot_general(
                    jnp.concatenate(left, 0), right, (((1,), (1,)), ((), ())), preferred_element_type=F32
                ).astype(BF16)
                mark = place((q - y) % N)
                for m in range(N):
                    first, second = jnp.where(k == 0, m, mark), jnp.where(k == 0, mark, m)
                    out_ref[first, second, t * tall : (t + 1) * tall, :] = result[m * tall : (m + 1) * tall]

    whole = pl.BlockSpec(memory_space=pltpu.VMEM)
    flat = [a for pair in others for a in pair]
    return pl.pallas_call(
        kernel,
        out_shape=jax.ShapeDtypeStruct((N, N, n * tall, H), BF16),
        in_specs=[whole] * (2 + len(flat)),
        out_specs=whole,
        compiler_params=pltpu.CompilerParams(vmem_limit_bytes=40 * 2**20),
        cost_estimate=pl.CostEstimate(flops=2 * 16 * n * tall * H * lat, bytes_accessed=2 * lat * rows * 4 * n, transcendentals=0),
        name="shares",
    )(mine, theirs, *flat)


def add(terms):
    total = terms[0].astype(F32)
    for term in terms[1:]:
        total = total + term.astype(F32)
    return total.astype(BF16)


def reduce(parts, stage):
    def where(z, k, x, y, n):
        return (z, k, x + n, y) if k == stage else (z, k, x, y + n)

    got = [send(parts[r], functools.partial(where, n=OFFSETS[r])) for r in range(N - 1)]
    return add([*got, parts[N - 1]])


def pick(stacked, index):
    return lax.dynamic_index_in_dim(stacked, index, 0, keepdims=False)


@functools.cache
def final_plan():
    edges = []
    for z, k, x, y in devices():
        late = (k + (1 if y >= 2 else 0)) % 2
        p = (y + (1 if x < z else 0) + late) % N
        edges.append(((z, k, x, y), (z, p // 2, x, y), p % 2, 0))
        if x == z and late == 0:
            edges.append(((z, k, x, y), (z, 1 - k, x, y), y % 2, 4))
        else:
            edges.append(((z, k, x, y), (x, y // 2, z, p), y % 2, 1))
    touching = {}
    for n, (source, target, _, _) in enumerate(edges):
        touching.setdefault(("from", source), []).append(n)
        touching.setdefault(("to", target), []).append(n)
    colour = {}
    for start in range(len(edges)):
        stack = [] if start in colour else [(start, 0)]
        while stack:
            n, c = stack.pop()
            if n in colour:
                assert colour[n] == c
                continue
            colour[n] = c
            for end in (("from", edges[n][0]), ("to", edges[n][1])):
                assert len(touching[end]) == 2
                stack.extend((m, 1 - c) for m in touching[end] if m != n)
    routes = [{}, {}]
    view = np.full((2 * N**3, 2), -1, np.int32)
    special = np.full((2 * N**3,), 2, np.int32)
    for n, (source, target, slot, kind) in enumerate(edges):
        c = colour[n]
        assert source not in routes[c] and view[linear(*target), slot] == -1
        routes[c][source] = target
        view[linear(*target), slot] = c + (2 if kind == 1 else kind)
        if kind == 4:
            special[linear(*source)] = c
    assert (view >= 0).all()
    return routes, np.concatenate([view, special[:, None]], 1)


def on_device(gradient, stat_old, inv_root):
    rows, lat = gradient.shape
    H = rows // 2
    Q = H // N
    z, k, x, y = (lax.axis_index(name) for name in AXES)

    def term(tile, turn, core):
        block = 2 * ((z + turn) % N) + core
        columns = lax.dynamic_slice_in_dim(inv_root, block * rows, rows, 1)
        return jnp.dot(columns, tile, preferred_element_type=F32)

    above = send(gradient, up(-1))
    below = send(gradient, up(1))
    partner = other_core(gradient)
    far = send(jnp.where(k == 0, below, above), lambda z, k, x, y: (z + 1 - 2 * k, k, x, y))
    above_partner, below_partner = other_core(jnp.stack([above, below]))
    far_partner = other_core(far)

    near = shares(gradient, partner, [(gradient, partner)], (0,), True)
    near = reduce(near, 0)
    near = reduce(near, 1)
    middle = shares(gradient, partner, [(above, above_partner), (below, below_partner)], (1, 3), False)
    middle = reduce(middle, 0)
    last = shares(gradient, partner, [(far, far_partner)], (2,), False)
    last = reduce(last, 0)
    middle = reduce(middle, 1)
    last = reduce(last, 1)

    product = term(gradient, 0, k) + term(partner, 0, 1 - k)
    product = product + (term(above, 1, k) + term(above_partner, 1, 1 - k))
    product = product + (term(below, 3, k) + term(below_partner, 3, 1 - k))
    product = product + (term(far, 2, k) + term(far_partner, 2, 1 - k))

    pieces = jnp.stack([near[:Q], middle[:Q], last, middle[Q:]])
    got = []
    for d in range(N):
        piece = jnp.concatenate([pick(pieces, (x + d - z) % N), near[Q:]], 0)
        got.append(send(piece, lambda z, k, x, y, d=d: (z, k, x + d, y)) if d else piece)
    got = jnp.stack(got)
    got = jnp.stack([pick(got, (x - c) % N) for c in range(N)])
    block = got[:, :Q].reshape(H, H)
    half = got[:, Q:].reshape(H // 2, H)

    routes, view = final_plan()
    here = jnp.asarray(view)[((z * 2 + k) * N + x) * N + y]
    padded = jnp.concatenate([half, half], 0)
    arrived = [send(jnp.where(here[2] == c, padded, block), lambda *device, c=c: routes[c][device]) for c in range(2)]
    stat = []
    for slot in range(2):
        which = here[slot]
        value = jnp.where(which % 2 == 0, arrived[0], arrived[1])
        diagonal = jnp.where(k == 0, jnp.concatenate([half, value[: H // 2]]), jnp.concatenate([value[: H // 2], half]))
        value = jnp.where(which >= 4, diagonal, jnp.where(which >= 2, value.T, value))
        stat.append(0.9 * stat_old[slot * H : (slot + 1) * H] + 0.1 * value.astype(F32))
    return jnp.concatenate(stat), product.astype(BF16)


def solution(mesh):
    fine = Mesh(mesh.devices.reshape(N, 2, N, N), AXES)
    row, col = ("z", "core"), ("x", "y")
    return jax.shard_map(
        on_device,
        mesh=fine,
        in_specs=(P(row, col), P(row, col), P(row, None)),
        out_specs=(P(row, col), P(row, col)),
        check_vma=False,
    )
```

```python
import functools

import jax
import jax.numpy as jnp
from jax import lax
from jax.experimental import pallas as pl
from jax.experimental.pallas import tpu as pltpu
from jax.sharding import Mesh
from jax.sharding import PartitionSpec as P

N = 4
AXES = ("z", "core", "x", "y")
OFFSETS = (1, 3, 2, 0)
F32 = jnp.float32
BF16 = jnp.bfloat16
VMEM = pl.BlockSpec(memory_space=pltpu.VMEM)
ANY = pl.BlockSpec(memory_space=pl.ANY)


def shift(z, j):
    return jnp.where(j < z, 1, 0)


def first_row(z, j, q):
    return (q + shift(z, j)) & 3


def row_of(z, k, j, q):
    u = first_row(z, j, q)
    return (u + (k ^ (u >> 1))) & 3


def mirrored_row(z, k, j, q):
    u = first_row(z, j, q)
    return jnp.where(z == j, (q + 2 + k) & 3, (u + 3 - (k ^ (u >> 1))) & 3)


def linear(z, k, x, y):
    return (((z % N) * 2 + k) * N + x % N) * N + y % N


def devices():
    return [(z, k, x, y) for z in range(N) for k in range(2) for x in range(N) for y in range(N)]


def send(value, where):
    pairs = [(linear(*device), where(*device)) for device in devices()]
    return lax.ppermute(value, AXES, [(source, linear(*to)) for source, to in pairs if to is not None])


def up(n):
    return lambda z, k, x, y: (z + n, k, x, y)


def other_core(value):
    return send(value, lambda z, k, x, y: (z, 1 - k, x, y))


def coordinates():
    return tuple(lax.axis_index(name) for name in AXES)


def call(kernel, outs, operands, after=(), specs=None, scratch=(), vmem=24):
    n = len(operands)

    def body(*refs):
        kernel(*refs[:n], *refs[n + len(after) :])

    return pl.pallas_call(
        body,
        out_shape=outs,
        in_specs=list(specs or [VMEM] * n) + [ANY] * len(after),
        out_specs=[VMEM] * len(outs),
        scratch_shapes=list(scratch),
        compiler_params=pltpu.CompilerParams(vmem_limit_bytes=vmem * 2**20),
        cost_estimate=pl.CostEstimate(flops=1, bytes_accessed=1, transcendentals=0),
    )(*operands, *after)


def array(*shape, dtype=BF16):
    return jax.ShapeDtypeStruct(shape, dtype)


def shares(mine, theirs, others, turns, diagonal, after=()):
    rows, lat = mine.shape
    H = rows // 2
    Q = H // N
    tall = Q + (Q // 2 if diagonal else 0)

    def kernel(mine_ref, theirs_ref, *refs):
        out_refs = refs[-N:]
        z, k, x, y = coordinates()

        def rows_of(block, part, parts):
            start = pl.multiple_of((block & 1) * H + part * (H // parts), H // parts)
            window = pl.ds(start, H // parts)
            return jnp.where((block >> 1) == k, mine_ref[window, :], theirs_ref[window, :])

        for t, turn in enumerate(turns):
            j = (z + turn) & 3
            for i, offset in enumerate(OFFSETS):
                q = (y + offset) & 3
                p = row_of(z, k, j, q)
                window = pl.ds(pl.multiple_of((q & 1) * H, H), H)
                right = jnp.where((q >> 1) == k, refs[2 * t][window, :], refs[2 * t + 1][window, :])
                left = []
                for offset in OFFSETS:
                    c = (x + offset) & 3
                    left.append(rows_of(p, c, N))
                    if diagonal:
                        left.append(rows_of((q + 2) & 3, k * N + c, 2 * N))
                result = lax.dot_general(
                    jnp.concatenate(left, 0), right, (((1,), (1,)), ((), ())), preferred_element_type=F32
                ).astype(BF16)
                here = slice(t * tall, (t + 1) * tall)

                @pl.when(k == 0)
                def _(result=result, i=i, here=here):
                    for m in range(N):
                        out_refs[m][i, here, :] = result[m * tall : (m + 1) * tall]

                @pl.when(k == 1)
                def _(result=result, i=i, here=here):
                    for m in range(N):
                        out_refs[i][m, here, :] = result[m * tall : (m + 1) * tall]

    n = len(turns)
    flat = [a for pair in others for a in pair]
    return call(kernel, [array(N, n * tall, H)] * N, [mine, theirs, *flat], after)


def multiply(inv_root, tiles, blocks, start, dtype, after=()):
    rows, lat = tiles[0].shape
    height = inv_root.shape[0]
    step = height // N

    def kernel(root_ref, *refs):
        tile_refs, refs = refs[: len(tiles)], refs[len(tiles) :]
        out_ref, held, sums, sems = refs[-4:]
        z, k, _, _ = coordinates()

        def copy(i):
            turn, whose = blocks[i]
            block = 2 * ((z + turn) & 3) + (k if whose == 0 else 1 - k)
            columns = pl.ds(pl.multiple_of(block * rows, rows), rows)
            return pltpu.make_async_copy(root_ref.at[:, columns], held.at[i], sems.at[i])

        copy(0).start()
        for i, tile_ref in enumerate(tile_refs):
            if i + 1 < len(tiles):
                copy(i + 1).start()
            copy(i).wait()
            for r in range(N):
                part = slice(r * step, (r + 1) * step)
                term = jnp.dot(held[i, part, :], tile_ref[...], preferred_element_type=F32)
                if i > 0:
                    term = term + sums[part, :]
                elif start is not None:
                    term = term + refs[0][part, :]
                if i + 1 < len(tiles):
                    sums[part, :] = term
                else:
                    out_ref[part, :] = term.astype(dtype)

    more = [] if start is None else [start]
    return call(
        kernel,
        [array(height, lat, dtype=dtype)],
        [inv_root, *tiles, *more],
        after,
        vmem=50,
        specs=[ANY] + [VMEM] * (len(tiles) + len(more)),
        scratch=[pltpu.VMEM((len(tiles), height, rows), BF16), pltpu.VMEM((height, lat), F32), pltpu.SemaphoreType.DMA((len(tiles),))],
    )[0]


def neighbours(above, below, after):
    def kernel(above_ref, below_ref, far_ref, both_ref):
        k = lax.axis_index("core")
        both_ref[0] = above_ref[...]
        both_ref[1] = below_ref[...]
        far_ref[...] = jnp.where(k == 0, below_ref[...], above_ref[...])

    return call(kernel, [array(*above.shape), array(2, *above.shape)], [above, below], after)


def scatter(parts, stage):
    def where(z, k, x, y, n):
        return (z, k, x + n, y) if k == stage else (z, k, x, y + n)

    return [send(parts[r], functools.partial(where, n=OFFSETS[r])) for r in range(N - 1)]


def total(got, own, after=()):
    def kernel(*refs):
        value = refs[N - 1][...].astype(F32)
        for ref in refs[: N - 1]:
            value = value + ref[...].astype(F32)
        value = value.astype(BF16)
        for r, ref in enumerate(refs[N:]):
            ref[...] = value[r] if own.ndim == 3 else value

    outs = [array(*own.shape[1:])] * N if own.ndim == 3 else [array(*own.shape)]
    return call(kernel, outs, [*got, own], after)


def hold(value, after):
    def kernel(value_ref, out_ref):
        out_ref[...] = value_ref[...]

    return call(kernel, [array(*value.shape)], [value], after)[0]


def step(k, n):
    return lambda z, core, x, y: (z, core, x + n, y) if core == k else (z, core, x, y + n)


def onward(parts):
    Q = parts[0].shape[1] // 2
    ahead = jnp.concatenate([parts[2][:, :Q], parts[0][:, Q:]], 1)
    back = jnp.concatenate([parts[1][:, :Q], parts[2][:, Q:]], 1)
    return send(ahead, step(0, 1)), send(back, step(0, -1))


def second_step(came, parts, after):
    Q = parts[0].shape[1] // 2

    def kernel(ahead_ref, back_ref, first_ref, second_ref, to_ref, fro_ref):
        to_ref[...] = (first_ref[:, :Q].astype(F32) + ahead_ref[:, :Q].astype(F32)).astype(BF16)
        fro_ref[...] = (second_ref[:, Q:].astype(F32) + back_ref[:, Q:].astype(F32)).astype(BF16)

    shape = (N, Q, parts[0].shape[2])
    to, fro = call(kernel, [array(*shape)] * 2, [*came, parts[0], parts[1]], after)
    return send(to, step(0, 1)), send(fro, step(0, -1))


def last_step(came, came_again, own, after):
    Q = own.shape[1] // 2

    def kernel(ahead_ref, back_ref, to_ref, fro_ref, own_ref, *out_refs):
        for r, ref in enumerate(out_refs):
            one = own_ref[r, :Q].astype(F32) + back_ref[r, :Q].astype(F32) + to_ref[r].astype(F32)
            two = own_ref[r, Q:].astype(F32) + ahead_ref[r, Q:].astype(F32) + fro_ref[r].astype(F32)
            ref[:Q, :] = one.astype(BF16)
            ref[Q:, :] = two.astype(BF16)

    return call(kernel, [array(*own.shape[1:])] * N, [*came, *came_again, own], after)


def mirror(turn):
    def where(z, k, x, y):
        j = (z + turn) % N
        u = (y + (j < z)) % N
        late = k ^ (u >> 1)
        p = (u + late) % N
        if turn == 0:
            return (z, 1, x, p) if late == 1 else None
        mirrored_u = (p + (z < j)) % N
        return (j, late ^ (mirrored_u >> 1), x, p)

    return where


def messages(near, middle, last, mirrored, other_half):
    Q = last.shape[0]
    H = last.shape[1]

    def kernel(near_ref, middle_ref, last_ref, m0_ref, m1_ref, m2_ref, m3_ref, half_ref, *out_refs):
        z, k, x, _ = coordinates()
        for d, out_ref in enumerate(out_refs):
            t = (x + d - z) & 3

            @pl.when(t == 0)
            def _(out_ref=out_ref):
                out_ref[:Q, :] = near_ref[:Q, :]
                out_ref[Q:, :] = jnp.where(k == 0, jnp.concatenate([near_ref[Q:, :], half_ref[...]], 0), m0_ref[...])

            for turn, (piece, mirrored_ref) in enumerate(
                ((middle_ref.at[:Q], m1_ref), (last_ref, m2_ref), (middle_ref.at[Q:], m3_ref)), 1
            ):

                @pl.when(t == turn)
                def _(out_ref=out_ref, piece=piece, mirrored_ref=mirrored_ref):
                    out_ref[:Q, :] = piece[...]
                    out_ref[Q:, :] = mirrored_ref[...]

    return call(kernel, [array(2 * Q, H)] * N, [near, middle, last, *mirrored, other_half])


def gathered(got):
    Q, H = got[0].shape[0] // 2, got[0].shape[1]

    def kernel(*refs):
        both_ref, wanted_ref = refs[N:]
        z, k, x, y = coordinates()
        for d in range(N):
            start = pl.multiple_of(((x - d) & 3) * Q, Q)
            for half in range(2):
                both_ref[half, pl.ds(start, Q), :] = refs[d][half * Q : (half + 1) * Q, :]
        stays = (row_of(z, k, x, y) >> 1) == k
        wanted_ref[...] = jnp.where(stays, both_ref[1], both_ref[0])

    return call(kernel, [array(2, H, H), array(H, H)], got)


def finish(both, arrived, stat_old):
    H = arrived.shape[0]
    E = H // 8

    def kernel(both_ref, arrived_ref, old_ref, out_ref):
        z, k, x, y = coordinates()

        def put(row, value):
            window = pl.ds(pl.multiple_of((row & 1) * H, H), H)
            out_ref[window, :] = 0.9 * old_ref[window, :] + 0.1 * value

        def turned(row, core, ref):
            whole = (z == x) & (core == 0)

            @pl.when(whole)
            def _():
                order = [2 * c + h for h in range(2) for c in range(N)]
                put(row, jnp.concatenate([ref[n * E : (n + 1) * E, :] for n in order], 0).astype(F32))

            @pl.when(jnp.logical_not(whole))
            def _():
                put(row, ref[...].astype(F32).T)

        plain, mirrored = row_of(z, k, x, y), mirrored_row(z, k, x, y)
        other_plain, other_mirrored = row_of(z, 1 - k, x, y), mirrored_row(z, 1 - k, x, y)

        @pl.when((plain >> 1) == k)
        def _():
            put(plain, both_ref[0].astype(F32))

        @pl.when((mirrored >> 1) == k)
        def _():
            turned(mirrored, k, both_ref.at[1])

        @pl.when((other_plain >> 1) == k)
        def _():
            put(other_plain, arrived_ref[...].astype(F32))

        @pl.when(((other_plain >> 1) != k) & ((other_mirrored >> 1) == k))
        def _():
            turned(other_mirrored, 1 - k, arrived_ref)

    return call(kernel, [array(2 * H, H, dtype=F32)], [both, arrived, stat_old])[0]


def on_device(gradient, stat_old, inv_root):
    Q = gradient.shape[0] // 8

    partner = other_core(gradient)
    above = send(gradient, up(-1))
    below = send(gradient, up(1))

    near = shares(gradient, partner, [(gradient, partner)], (0,), True)
    near_came = scatter(near, 0)
    product = multiply(inv_root, [gradient, partner], [(0, 0), (0, 1)], None, F32, [near[0]])

    far, both = neighbours(above, below, [product, *near_came])
    far = send(far, lambda z, k, x, y: (z + 1 - 2 * k, k, x, y))
    above_partner, below_partner = other_core(both)
    near = total(near_came, near[3], [both])
    near_came = scatter(near, 1)

    middle = shares(gradient, partner, [(above, above_partner), (below, below_partner)], (1, 3), False, [near[0]])
    middle_came = onward(middle)
    (near,) = total(near_came, near[3], [middle[0]])
    mirrored = [send(near[:Q], mirror(0)), None, None, None]
    other_half = send(near[Q:], lambda z, k, x, y: (z, 0, x, y) if k == 1 else None)

    far = hold(far, [near])
    far_partner = other_core(far)
    last = shares(gradient, partner, [(far, far_partner)], (2,), False)
    last_came = scatter(last, 0)
    product = multiply(
        inv_root, [above, above_partner, below, below_partner], [(1, 0), (1, 1), (3, 0), (3, 1)], product, F32, [last[0]]
    )
    middle_again = second_step(middle_came, middle, [product])
    product = multiply(inv_root, [far, far_partner], [(2, 0), (2, 1)], product, BF16, [last[0]])

    middle = last_step(middle_came, middle_again, middle[3], [product])
    middle_came = scatter(middle, 1)
    last = total(last_came, last[3], [middle[0], mirrored[0], other_half])
    last_came = scatter(last, 1)
    (middle,) = total(middle_came, middle[3], [last[0]])
    mirrored[3] = send(middle[:Q], mirror(1))
    mirrored[1] = send(middle[Q:], mirror(3))
    (last,) = total(last_came, last[3], [mirrored[1], mirrored[3]])
    mirrored[2] = send(last, mirror(2))

    out = messages(near, middle, last, mirrored, other_half)
    got = [out[0]] + [send(out[d], lambda z, k, x, y, d=d: (z, k, x + d, y)) for d in range(1, N)]
    both, wanted = gathered(got)
    return finish(both, other_core(wanted), stat_old), product


def solution(mesh):
    fine = Mesh(mesh.devices.reshape(N, 2, N, N), AXES)
    row, col = ("z", "core"), ("x", "y")
    return jax.shard_map(
        on_device,
        mesh=fine,
        in_specs=(P(row, col), P(row, col), P(row, None)),
        out_specs=(P(row, col), P(row, col)),
        check_vma=False,
    )
```

```python
import functools

import jax
import jax.numpy as jnp
from jax import lax
from jax.experimental import pallas as pl
from jax.experimental.pallas import tpu as pltpu
from jax.sharding import Mesh
from jax.sharding import PartitionSpec as P

N = 4
AXES = ("z", "core", "x", "y")
OFFSETS = (1, 3, 2, 0)
F32 = jnp.float32
BF16 = jnp.bfloat16
VMEM = pl.BlockSpec(memory_space=pltpu.VMEM)
ANY = pl.BlockSpec(memory_space=pl.ANY)


def shift(z, j):
    return jnp.where(j < z, 1, 0)


def first_row(z, j, q):
    return (q + shift(z, j)) & 3


def row_of(z, k, j, q):
    u = first_row(z, j, q)
    return (u + (k ^ (u >> 1))) & 3


def mirrored_row(z, k, j, q):
    u = first_row(z, j, q)
    return jnp.where(z == j, (q + 2 + k) & 3, (u + 3 - (k ^ (u >> 1))) & 3)


def linear(z, k, x, y):
    return (((z % N) * 2 + k) * N + x % N) * N + y % N


def devices():
    return [(z, k, x, y) for z in range(N) for k in range(2) for x in range(N) for y in range(N)]


def send(value, where):
    pairs = [(linear(*device), where(*device)) for device in devices()]
    return lax.ppermute(value, AXES, [(source, linear(*to)) for source, to in pairs if to is not None])


def up(n):
    return lambda z, k, x, y: (z + n, k, x, y)


def other_core(value):
    return send(value, lambda z, k, x, y: (z, 1 - k, x, y))


def coordinates():
    return tuple(lax.axis_index(name) for name in AXES)


def call(kernel, outs, operands, after=(), specs=None, scratch=(), vmem=24):
    n = len(operands)

    def body(*refs):
        kernel(*refs[:n], *refs[n + len(after) :])

    return pl.pallas_call(
        body,
        out_shape=outs,
        in_specs=list(specs or [VMEM] * n) + [ANY] * len(after),
        out_specs=[VMEM] * len(outs),
        scratch_shapes=list(scratch),
        compiler_params=pltpu.CompilerParams(vmem_limit_bytes=vmem * 2**20),
        cost_estimate=pl.CostEstimate(flops=1, bytes_accessed=1, transcendentals=0),
    )(*operands, *after)


def array(*shape, dtype=BF16):
    return jax.ShapeDtypeStruct(shape, dtype)


def shares(mine, theirs, others, turns, diagonal, places, after=()):
    rows, lat = mine.shape
    H = rows // 2
    Q = H // N
    tall = Q + (Q // 2 if diagonal else 0)

    def kernel(mine_ref, theirs_ref, *refs):
        out_refs = refs[2 * len(turns) :]
        z, k, x, y = coordinates()

        def rows_of(block, part, parts):
            start = pl.multiple_of((block & 1) * H + part * (H // parts), H // parts)
            window = pl.ds(start, H // parts)
            return jnp.where((block >> 1) == k, mine_ref[window, :], theirs_ref[window, :])

        for t, turn in enumerate(turns):
            j = (z + turn) & 3
            for i, offset in enumerate(OFFSETS):
                q = (y + offset) & 3
                p = row_of(z, k, j, q)
                window = pl.ds(pl.multiple_of((q & 1) * H, H), H)
                right = jnp.where((q >> 1) == k, refs[2 * t][window, :], refs[2 * t + 1][window, :])
                left = []
                for offset in OFFSETS:
                    c = (x + offset) & 3
                    left.append(rows_of(p, c, N))
                    if diagonal:
                        left.append(rows_of((q + 2) & 3, k * N + c, 2 * N))
                result = lax.dot_general(
                    jnp.concatenate(left, 0), right, (((1,), (1,)), ((), ())), preferred_element_type=F32
                ).astype(BF16)
                @pl.when(k == 0)
                def _(result=result, i=i, t=t):
                    for m in range(N):
                        for out, to, start, size in places[m][t]:
                            rows_sent = slice(m * tall + start, m * tall + start + size)
                            out_refs[out][i, to : to + size, :] = result[rows_sent]

                @pl.when(k == 1)
                def _(result=result, i=i, t=t):
                    for m in range(N):
                        for out, to, start, size in places[i][t]:
                            rows_sent = slice(m * tall + start, m * tall + start + size)
                            out_refs[out][m, to : to + size, :] = result[rows_sent]

    flat = [a for pair in others for a in pair]
    heights = {}
    for spots in places:
        for out, to, _, size in (piece for pieces in spots for piece in pieces):
            heights[out] = max(heights.get(out, 0), to + size)
    return call(kernel, [array(N, heights[out], H) for out in sorted(heights)], [mine, theirs, *flat], after)


def multiply(inv_root, tiles, blocks, start, dtype, after=()):
    rows, lat = tiles[0].shape
    height = inv_root.shape[0]
    step = height // N

    def kernel(root_ref, *refs):
        tile_refs, refs = refs[: len(tiles)], refs[len(tiles) :]
        out_ref, token_ref, held, sums, sems = refs[-5:]
        token_ref[...] = jnp.zeros_like(token_ref)
        z, k, _, _ = coordinates()

        def copy(i):
            turn, whose = blocks[i]
            block = 2 * ((z + turn) & 3) + (k if whose == 0 else 1 - k)
            columns = pl.ds(pl.multiple_of(block * rows, rows), rows)
            return pltpu.make_async_copy(root_ref.at[:, columns], held.at[i], sems.at[i])

        copy(0).start()
        for i, tile_ref in enumerate(tile_refs):
            if i + 1 < len(tiles):
                copy(i + 1).start()
            copy(i).wait()
            for r in range(N):
                part = slice(r * step, (r + 1) * step)
                term = jnp.dot(held[i, part, :], tile_ref[...], preferred_element_type=F32)
                if i > 0:
                    term = term + sums[part, :]
                elif start is not None:
                    term = term + refs[0][part, :]
                if i + 1 < len(tiles):
                    sums[part, :] = term
                else:
                    out_ref[part, :] = term.astype(dtype)

    more = [] if start is None else [start]
    return call(
        kernel,
        [array(height, lat, dtype=dtype), array(8, 128, dtype=F32)],
        [inv_root, *tiles, *more],
        after,
        vmem=50,
        specs=[ANY] + [VMEM] * (len(tiles) + len(more)),
        scratch=[pltpu.VMEM((len(tiles), height, rows), BF16), pltpu.VMEM((height, lat), F32), pltpu.SemaphoreType.DMA((len(tiles),))],
    )


def neighbours(above, below, after):
    def kernel(above_ref, below_ref, far_ref, both_ref):
        k = lax.axis_index("core")
        both_ref[0] = above_ref[...]
        both_ref[1] = below_ref[...]
        far_ref[...] = jnp.where(k == 0, below_ref[...], above_ref[...])

    return call(kernel, [array(*above.shape), array(2, *above.shape)], [above, below], after)


def scatter(parts, stage):
    def where(z, k, x, y, n):
        return (z, k, x + n, y) if k == stage else (z, k, x, y + n)

    return [send(parts[r], functools.partial(where, n=OFFSETS[r])) for r in range(N - 1)]


def total(got, own, after=()):
    def kernel(*refs):
        value = refs[N - 1][...].astype(F32)
        for ref in refs[: N - 1]:
            value = value + ref[...].astype(F32)
        value = value.astype(BF16)
        for r, ref in enumerate(refs[N:]):
            ref[...] = value[r] if own.ndim == 3 else value

    outs = [array(*own.shape[1:])] * N if own.ndim == 3 else [array(*own.shape)]
    return call(kernel, outs, [*got, own], after)


def hold(value, after):
    def kernel(value_ref, out_ref):
        out_ref[...] = value_ref[...]

    return call(kernel, [array(*value.shape)], [value], after)[0]


def step(k, n):
    return lambda z, core, x, y: (z, core, x + n, y) if core == k else (z, core, x, y + n)


def second_step(came, first, second, far_came, far_first, far_second, after):
    Q, h = first.shape[1], far_first.shape[1]

    def kernel(ahead_ref, back_ref, first_ref, second_ref, ahead2_ref, back2_ref, first2_ref, second2_ref, to_ref, fro_ref):
        to_ref[:, :Q] = (first_ref[...].astype(F32) + ahead_ref[:, :Q].astype(F32)).astype(BF16)
        fro_ref[:, :Q] = (second_ref[...].astype(F32) + back_ref[:, Q:].astype(F32)).astype(BF16)
        to_ref[:, Q:] = (first2_ref[...].astype(F32) + ahead2_ref[:, :h].astype(F32)).astype(BF16)
        fro_ref[:, Q:] = (second2_ref[...].astype(F32) + back2_ref[:, h:].astype(F32)).astype(BF16)

    shape = array(first.shape[0], Q + h, first.shape[2])
    to, fro = call(kernel, [shape] * 2, [*came, first, second, *far_came, far_first, far_second], after)
    return send(to, step(0, 1)), send(fro, step(0, -1))


def last_step(came, own, far_came, far_own, came_again, after):
    Q = far_own.shape[1]
    h = Q // 2

    def kernel(ahead_ref, back_ref, own_ref, ahead2_ref, back2_ref, own2_ref, to_ref, fro_ref, *out_refs):
        def put(ref, at, *terms):
            value = terms[0].astype(F32)
            for term in terms[1:]:
                value = value + term.astype(F32)
            ref[at : at + terms[0].shape[0], :] = value.astype(BF16)

        for r, ref in enumerate(out_refs):
            put(ref, 0, own_ref[r, :Q], back_ref[r, :Q], to_ref[r, :Q])
            put(ref, Q, own_ref[r, Q:], ahead_ref[r, Q:], fro_ref[r, :Q])
            put(ref, 2 * Q, own2_ref[r, :h], back2_ref[r, :h], to_ref[r, Q:])
            put(ref, 2 * Q + h, own2_ref[r, h:], ahead2_ref[r, h:], fro_ref[r, Q:])

    outs = [array(3 * Q, own.shape[2])] * N
    return call(kernel, outs, [*came, own, *far_came, far_own, *came_again], after)


def mirror(turn):
    def where(z, k, x, y):
        j = (z + turn) % N
        u = (y + (j < z)) % N
        late = k ^ (u >> 1)
        p = (u + late) % N
        if turn == 0:
            return (z, 1, x, p) if late == 1 else None
        mirrored_u = (p + (z < j)) % N
        return (j, late ^ (mirrored_u >> 1), x, p)

    return where


def messages(near, middle, last, mirrored, other_half):
    Q = last.shape[0]
    H = last.shape[1]

    def kernel(near_ref, middle_ref, last_ref, m0_ref, m1_ref, m2_ref, m3_ref, half_ref, *out_refs):
        z, k, x, _ = coordinates()
        for d, out_ref in enumerate(out_refs):
            t = (x + d - z) & 3

            @pl.when(t == 0)
            def _(out_ref=out_ref):
                out_ref[:Q, :] = near_ref[:Q, :]
                out_ref[Q:, :] = jnp.where(k == 0, jnp.concatenate([near_ref[Q:, :], half_ref[...]], 0), m0_ref[...])

            for turn, (piece, mirrored_ref) in enumerate(
                ((middle_ref.at[:Q], m1_ref), (last_ref, m2_ref), (middle_ref.at[Q:], m3_ref)), 1
            ):

                @pl.when(t == turn)
                def _(out_ref=out_ref, piece=piece, mirrored_ref=mirrored_ref):
                    out_ref[:Q, :] = piece[...]
                    out_ref[Q:, :] = mirrored_ref[...]

    return call(kernel, [array(2 * Q, H)] * N, [near, middle, last, *mirrored, other_half])


def gathered(got, after):
    Q, H = got[0].shape[0] // 2, got[0].shape[1]

    def kernel(*refs):
        both_ref, wanted_ref = refs[N:]
        z, k, x, y = coordinates()
        for d in range(N):
            start = pl.multiple_of(((x - d) & 3) * Q, Q)
            for half in range(2):
                both_ref[half, pl.ds(start, Q), :] = refs[d][half * Q : (half + 1) * Q, :]
        stays = (row_of(z, k, x, y) >> 1) == k
        wanted_ref[...] = jnp.where(stays, both_ref[1], both_ref[0])

    return call(kernel, [array(2, H, H), array(H, H)], got, after)


def finish(both, arrived, stat_old):
    H = arrived.shape[0]
    E = H // 8

    def kernel(both_ref, arrived_ref, old_ref, out_ref):
        z, k, x, y = coordinates()

        def put(row, value):
            window = pl.ds(pl.multiple_of((row & 1) * H, H), H)
            out_ref[window, :] = 0.9 * old_ref[window, :] + 0.1 * value

        def turned(row, core, ref):
            whole = (z == x) & (core == 0)

            @pl.when(whole)
            def _():
                order = [2 * c + h for h in range(2) for c in range(N)]
                put(row, jnp.concatenate([ref[n * E : (n + 1) * E, :] for n in order], 0).astype(F32))

            @pl.when(jnp.logical_not(whole))
            def _():
                put(row, ref[...].astype(F32).T)

        plain, mirrored = row_of(z, k, x, y), mirrored_row(z, k, x, y)
        other_plain, other_mirrored = row_of(z, 1 - k, x, y), mirrored_row(z, 1 - k, x, y)

        @pl.when((plain >> 1) == k)
        def _():
            put(plain, both_ref[0].astype(F32))

        @pl.when((mirrored >> 1) == k)
        def _():
            turned(mirrored, k, both_ref.at[1])

        @pl.when((other_plain >> 1) == k)
        def _():
            put(other_plain, arrived_ref[...].astype(F32))

        @pl.when(((other_plain >> 1) != k) & ((other_mirrored >> 1) == k))
        def _():
            turned(other_mirrored, 1 - k, arrived_ref)

    return call(kernel, [array(2 * H, H, dtype=F32)], [both, arrived, stat_old])[0]


def on_device(gradient, stat_old, inv_root):
    Q = gradient.shape[0] // 8

    partner = other_core(gradient)
    above = send(gradient, up(-1))
    below = send(gradient, up(1))

    tall = Q + Q // 2
    straight = [[[(r, 0, 0, tall)]] for r in range(N)]
    h = Q // 2
    halved = [
        [[(2, 0, 0, h), (0, h, h, h)]],
        [[(1, 0, 0, h), (3, 0, h, h)]],
        [[(0, 0, 0, h), (1, h, h, h)]],
        [[(4, 0, 0, Q)]],
    ]
    by_plane = [
        [[(2, 0, 0, Q)], [(0, Q, 0, Q)]],
        [[(1, 0, 0, Q)], [(3, 0, 0, Q)]],
        [[(0, 0, 0, Q)], [(1, Q, 0, Q)]],
        [[(4, 0, 0, Q)], [(4, Q, 0, Q)]],
    ]
    near = shares(gradient, partner, [(gradient, partner)], (0,), True, straight)
    near_came = scatter(near, 0)
    product, token = multiply(inv_root, [gradient, partner], [(0, 0), (0, 1)], None, F32, [near[0]])

    far, both = neighbours(above, below, [token, *near_came])
    far = send(far, lambda z, k, x, y: (z + 1 - 2 * k, k, x, y))
    above_partner, below_partner = other_core(both)
    near = total(near_came, near[3], [both])
    near_came = scatter(near, 1)

    ahead, back, first, second, own = shares(
        gradient,
        partner,
        [(above, above_partner), (below, below_partner)],
        (1, 3),
        False,
        by_plane,
        [near[0]],
    )
    came = send(ahead, step(0, 1)), send(back, step(0, -1))
    (near,) = total(near_came, near[3], [ahead])

    other_half = send(near[Q:], lambda z, k, x, y: (z, 0, x, y) if k == 1 else None)
    far = hold(far, [near])
    far_partner = other_core(far)
    ahead, back, far_first, far_second, far_own = shares(
        gradient, partner, [(far, far_partner)], (2,), False, halved, [ahead]
    )
    far_came = send(ahead, step(0, 1)), send(back, step(0, -1))
    product, token = multiply(inv_root, [far, far_partner], [(2, 0), (2, 1)], product, F32, [ahead, other_half])
    came_again = second_step(came, first, second, far_came, far_first, far_second, [token])
    mirrored = [send(near[:Q], mirror(0))]
    product, token = multiply(
        inv_root, [above, above_partner], [(1, 0), (1, 1)], product, F32, [*came, *far_came, token]
    )
    rest = last_step(came, own, far_came, far_own, came_again, [token, mirrored[0]])
    (rest,) = total(scatter(rest, 1), rest[3])

    mirrored += [
        send(rest[Q : 2 * Q], mirror(3)),
        send(rest[2 * Q :], mirror(2)),
        send(rest[:Q], mirror(1)),
    ]
    out = messages(near, rest[: 2 * Q], rest[2 * Q :], mirrored, other_half)
    got = [out[0]] + [send(out[d], lambda z, k, x, y, d=d: (z, k, x + d, y)) for d in range(1, N)]
    product, token = multiply(inv_root, [below, below_partner], [(3, 0), (3, 1)], product, BF16, [out[0]])
    both, wanted = gathered(got, [token])
    return finish(both, other_core(wanted), stat_old), product


def solution(mesh):
    fine = Mesh(mesh.devices.reshape(N, 2, N, N), AXES)
    row, col = ("z", "core"), ("x", "y")
    return jax.shard_map(
        on_device,
        mesh=fine,
        in_specs=(P(row, col), P(row, col), P(row, None)),
        out_specs=(P(row, col), P(row, col)),
        check_vma=False,
    )
```

```python
import functools

import jax
import jax.numpy as jnp
from jax import lax
from jax.experimental import pallas as pl
from jax.experimental.pallas import tpu as pltpu
from jax.sharding import Mesh
from jax.sharding import PartitionSpec as P

N = 4
AXES = ("z", "core", "x", "y")
OFFSETS = (1, 3, 2, 0)
F32 = jnp.float32
BF16 = jnp.bfloat16
VMEM = pl.BlockSpec(memory_space=pltpu.VMEM)
ANY = pl.BlockSpec(memory_space=pl.ANY)


def shift(z, j):
    return jnp.where(j < z, 1, 0)


def first_row(z, j, q):
    return (q + shift(z, j)) & 3


def row_of(z, k, j, q):
    u = first_row(z, j, q)
    return (u + (k ^ (u >> 1))) & 3


def mirrored_row(z, k, j, q):
    u = first_row(z, j, q)
    return jnp.where(z == j, (q + 2 + k) & 3, (u + 3 - (k ^ (u >> 1))) & 3)


def linear(z, k, x, y):
    return (((z % N) * 2 + k) * N + x % N) * N + y % N


def devices():
    return [(z, k, x, y) for z in range(N) for k in range(2) for x in range(N) for y in range(N)]


def send(value, where):
    pairs = [(linear(*device), where(*device)) for device in devices()]
    return lax.ppermute(value, AXES, [(source, linear(*to)) for source, to in pairs if to is not None])


def up(n):
    return lambda z, k, x, y: (z + n, k, x, y)


def other_core(value):
    return send(value, lambda z, k, x, y: (z, 1 - k, x, y))


def coordinates():
    return tuple(lax.axis_index(name) for name in AXES)


def call(kernel, outs, operands, after=(), specs=None, scratch=(), vmem=24):
    n = len(operands)

    def body(*refs):
        kernel(*refs[:n], *refs[n + len(after) :])

    return pl.pallas_call(
        body,
        out_shape=outs,
        in_specs=list(specs or [VMEM] * n) + [ANY] * len(after),
        out_specs=[VMEM] * len(outs),
        scratch_shapes=list(scratch),
        compiler_params=pltpu.CompilerParams(vmem_limit_bytes=vmem * 2**20),
        cost_estimate=pl.CostEstimate(flops=1, bytes_accessed=1, transcendentals=0),
    )(*operands, *after)


def array(*shape, dtype=BF16):
    return jax.ShapeDtypeStruct(shape, dtype)


def shares(mine, theirs, others, turns, diagonal, places, after=()):
    rows, lat = mine.shape
    H = rows // 2
    Q = H // N
    tall = Q + (Q // 2 if diagonal else 0)

    def kernel(mine_ref, theirs_ref, *refs):
        out_refs = refs[2 * len(turns) :]
        z, k, x, y = coordinates()

        def rows_of(block, part, parts):
            start = pl.multiple_of((block & 1) * H + part * (H // parts), H // parts)
            window = pl.ds(start, H // parts)
            return jnp.where((block >> 1) == k, mine_ref[window, :], theirs_ref[window, :])

        def work(core):
            for t, turn in enumerate(turns):
                j = (z + turn) & 3
                for i, offset in enumerate(OFFSETS):
                    q = (y + offset) & 3
                    p = row_of(z, k, j, q)
                    window = pl.ds(pl.multiple_of((q & 1) * H, H), H)
                    right = jnp.where((q >> 1) == k, refs[2 * t][window, :], refs[2 * t + 1][window, :])
                    left = []
                    for offset in OFFSETS:
                        c = (x + offset) & 3
                        left.append(rows_of(p, c, N))
                        if diagonal:
                            left.append(rows_of((q + 2) & 3, k * N + c, 2 * N))
                    result = lax.dot_general(
                        jnp.concatenate(left, 0), right, (((1,), (1,)), ((), ())), preferred_element_type=F32
                    ).astype(BF16)
                    for m in range(N):
                        part, second = (m, i) if core == 0 else (i, m)
                        for out, to, start, size in places[part][t]:
                            rows_sent = slice(m * tall + start, m * tall + start + size)
                            out_refs[out][second, to : to + size, :] = result[rows_sent]

        for core in range(2):
            pl.when(k == core)(functools.partial(work, core))

    flat = [a for pair in others for a in pair]
    heights = {}
    for spots in places:
        for out, to, _, size in (piece for pieces in spots for piece in pieces):
            heights[out] = max(heights.get(out, 0), to + size)
    return call(kernel, [array(N, heights[out], H) for out in sorted(heights)], [mine, theirs, *flat], after)


def multiply(inv_root, tiles, blocks, start, dtype, after=()):
    rows, lat = tiles[0].shape
    height = inv_root.shape[0]
    step = height // N

    def kernel(root_ref, *refs):
        tile_refs, refs = refs[: len(tiles)], refs[len(tiles) :]
        out_ref, token_ref, held, sums, sems = refs[-5:]
        token_ref[...] = jnp.zeros_like(token_ref)
        z, k, _, _ = coordinates()

        def copy(i):
            turn, whose = blocks[i]
            block = 2 * ((z + turn) & 3) + (k if whose == 0 else 1 - k)
            columns = pl.ds(pl.multiple_of(block * rows, rows), rows)
            return pltpu.make_async_copy(root_ref.at[:, columns], held.at[i], sems.at[i])

        copy(0).start()
        for i, tile_ref in enumerate(tile_refs):
            if i + 1 < len(tiles):
                copy(i + 1).start()
            copy(i).wait()
            for r in range(N):
                part = slice(r * step, (r + 1) * step)
                term = jnp.dot(held[i, part, :], tile_ref[...], preferred_element_type=F32)
                if i > 0:
                    term = term + sums[part, :]
                elif start is not None:
                    term = term + refs[0][part, :]
                if i + 1 < len(tiles):
                    sums[part, :] = term
                else:
                    out_ref[part, :] = term.astype(dtype)

    more = [] if start is None else [start]
    return call(
        kernel,
        [array(height, lat, dtype=dtype), array(8, 128, dtype=F32)],
        [inv_root, *tiles, *more],
        after,
        vmem=42,
        specs=[ANY] + [VMEM] * (len(tiles) + len(more)),
        scratch=[pltpu.VMEM((len(tiles), height, rows), BF16), pltpu.VMEM((height, lat), F32), pltpu.SemaphoreType.DMA((len(tiles),))],
    )


def neighbours(above, below, after):
    def kernel(above_ref, below_ref, far_ref, both_ref):
        k = lax.axis_index("core")
        both_ref[0] = above_ref[...]
        both_ref[1] = below_ref[...]
        far_ref[...] = jnp.where(k == 0, below_ref[...], above_ref[...])

    return call(kernel, [array(*above.shape), array(2, *above.shape)], [above, below], after)


def scatter(parts, stage):
    def where(z, k, x, y, n):
        return (z, k, x + n, y) if k == stage else (z, k, x, y + n)

    return [send(parts[r], functools.partial(where, n=OFFSETS[r])) for r in range(N - 1)]


def total(got, own, after=()):
    def kernel(*refs):
        value = refs[N - 1][...].astype(F32)
        for ref in refs[: N - 1]:
            value = value + ref[...].astype(F32)
        value = value.astype(BF16)
        for r, ref in enumerate(refs[N:]):
            ref[...] = value[r] if own.ndim == 3 else value

    outs = [array(*own.shape[1:])] * N if own.ndim == 3 else [array(*own.shape)]
    return call(kernel, outs, [*got, own], after)


def hold(value, after):
    def kernel(value_ref, out_ref):
        out_ref[...] = value_ref[...]

    return call(kernel, [array(*value.shape)], [value], after)[0]


def step(k, n):
    return lambda z, core, x, y: (z, core, x + n, y) if core == k else (z, core, x, y + n)


def second_step(came, first, second, far_came, far_first, far_second, after):
    Q, h = first.shape[1], far_first.shape[1]

    def kernel(ahead_ref, back_ref, first_ref, second_ref, ahead2_ref, back2_ref, first2_ref, second2_ref, to_ref, fro_ref):
        to_ref[:, :Q] = (first_ref[...].astype(F32) + ahead_ref[:, :Q].astype(F32)).astype(BF16)
        fro_ref[:, :Q] = (second_ref[...].astype(F32) + back_ref[:, Q:].astype(F32)).astype(BF16)
        to_ref[:, Q:] = (first2_ref[...].astype(F32) + ahead2_ref[:, :h].astype(F32)).astype(BF16)
        fro_ref[:, Q:] = (second2_ref[...].astype(F32) + back2_ref[:, h:].astype(F32)).astype(BF16)

    shape = array(first.shape[0], Q + h, first.shape[2])
    to, fro = call(kernel, [shape] * 2, [*came, first, second, *far_came, far_first, far_second], after)
    return send(to, step(0, 1)), send(fro, step(0, -1))


def last_step(came, own, far_came, far_own, came_again, after):
    Q = far_own.shape[1]
    h = Q // 2

    def kernel(ahead_ref, back_ref, own_ref, ahead2_ref, back2_ref, own2_ref, to_ref, fro_ref, *out_refs):
        def put(ref, at, *terms):
            value = terms[0].astype(F32)
            for term in terms[1:]:
                value = value + term.astype(F32)
            ref[at : at + terms[0].shape[0], :] = value.astype(BF16)

        for r, ref in enumerate(out_refs):
            put(ref, 0, own_ref[r, :Q], back_ref[r, :Q], to_ref[r, :Q])
            put(ref, Q, own_ref[r, Q:], ahead_ref[r, Q:], fro_ref[r, :Q])
            put(ref, 2 * Q, own2_ref[r, :h], back2_ref[r, :h], to_ref[r, Q:])
            put(ref, 2 * Q + h, own2_ref[r, h:], ahead2_ref[r, h:], fro_ref[r, Q:])

    outs = [array(3 * Q, own.shape[2])] * N
    return call(kernel, outs, [*came, own, *far_came, far_own, *came_again], after)


def mirror(turn):
    def where(z, k, x, y):
        j = (z + turn) % N
        u = (y + (j < z)) % N
        late = k ^ (u >> 1)
        p = (u + late) % N
        if turn == 0:
            return (z, 1, x, p) if late == 1 else None
        mirrored_u = (p + (z < j)) % N
        return (j, late ^ (mirrored_u >> 1), x, p)

    return where


def messages(near, middle, last, mirrored, other_half):
    Q = last.shape[0]
    H = last.shape[1]

    def kernel(near_ref, middle_ref, last_ref, m0_ref, m1_ref, m2_ref, m3_ref, half_ref, *out_refs):
        z, k, x, _ = coordinates()
        for d, out_ref in enumerate(out_refs):
            t = (x + d - z) & 3

            @pl.when(t == 0)
            def _(out_ref=out_ref):
                out_ref[:Q, :] = near_ref[:Q, :]
                out_ref[Q:, :] = jnp.where(k == 0, jnp.concatenate([near_ref[Q:, :], half_ref[...]], 0), m0_ref[...])

            for turn, (piece, mirrored_ref) in enumerate(
                ((middle_ref.at[:Q], m1_ref), (last_ref, m2_ref), (middle_ref.at[Q:], m3_ref)), 1
            ):

                @pl.when(t == turn)
                def _(out_ref=out_ref, piece=piece, mirrored_ref=mirrored_ref):
                    out_ref[:Q, :] = piece[...]
                    out_ref[Q:, :] = mirrored_ref[...]

    return call(kernel, [array(2 * Q, H)] * N, [near, middle, last, *mirrored, other_half])


def gathered(got, after):
    Q, H = got[0].shape[0] // 2, got[0].shape[1]

    def kernel(*refs):
        both_ref, wanted_ref = refs[N:]
        z, k, x, y = coordinates()
        for d in range(N):
            start = pl.multiple_of(((x - d) & 3) * Q, Q)
            for half in range(2):
                both_ref[half, pl.ds(start, Q), :] = refs[d][half * Q : (half + 1) * Q, :]
        stays = (row_of(z, k, x, y) >> 1) == k
        wanted_ref[...] = jnp.where(stays, both_ref[1], both_ref[0])

    return call(kernel, [array(2, H, H), array(H, H)], got, after)


def finish(both, arrived, stat_old):
    H = arrived.shape[0]
    E = H // 8

    def kernel(both_ref, arrived_ref, old_ref, out_ref):
        z, k, x, y = coordinates()

        def put(row, value):
            window = pl.ds(pl.multiple_of((row & 1) * H, H), H)
            out_ref[window, :] = 0.9 * old_ref[window, :] + 0.1 * value

        def turned(row, core, ref):
            whole = (z == x) & (core == 0)

            @pl.when(whole)
            def _():
                order = [2 * c + h for h in range(2) for c in range(N)]
                put(row, jnp.concatenate([ref[n * E : (n + 1) * E, :] for n in order], 0).astype(F32))

            @pl.when(jnp.logical_not(whole))
            def _():
                put(row, ref[...].astype(F32).T)

        plain, mirrored = row_of(z, k, x, y), mirrored_row(z, k, x, y)
        other_plain, other_mirrored = row_of(z, 1 - k, x, y), mirrored_row(z, 1 - k, x, y)

        @pl.when((plain >> 1) == k)
        def _():
            put(plain, both_ref[0].astype(F32))

        @pl.when((mirrored >> 1) == k)
        def _():
            turned(mirrored, k, both_ref.at[1])

        @pl.when((other_plain >> 1) == k)
        def _():
            put(other_plain, arrived_ref[...].astype(F32))

        @pl.when(((other_plain >> 1) != k) & ((other_mirrored >> 1) == k))
        def _():
            turned(other_mirrored, 1 - k, arrived_ref)

    return call(kernel, [array(2 * H, H, dtype=F32)], [both, arrived, stat_old])[0]


def on_device(gradient, stat_old, inv_root):
    Q = gradient.shape[0] // 8

    partner = other_core(gradient)
    above = send(gradient, up(-1))
    below = send(gradient, up(1))

    tall = Q + Q // 2
    straight = [[[(r, 0, 0, tall)]] for r in range(N)]
    h = Q // 2
    halved = [
        [[(2, 0, 0, h), (0, h, h, h)]],
        [[(1, 0, 0, h), (3, 0, h, h)]],
        [[(0, 0, 0, h), (1, h, h, h)]],
        [[(4, 0, 0, Q)]],
    ]
    by_plane = [
        [[(2, 0, 0, Q)], [(0, Q, 0, Q)]],
        [[(1, 0, 0, Q)], [(3, 0, 0, Q)]],
        [[(0, 0, 0, Q)], [(1, Q, 0, Q)]],
        [[(4, 0, 0, Q)], [(4, Q, 0, Q)]],
    ]
    near = shares(gradient, partner, [(gradient, partner)], (0,), True, straight)
    near_came = scatter(near, 0)
    product, token = multiply(inv_root, [gradient, partner], [(0, 0), (0, 1)], None, F32, [near[0]])

    far, both = neighbours(above, below, [token, *near_came])
    far = send(far, lambda z, k, x, y: (z + 1 - 2 * k, k, x, y))
    above_partner, below_partner = other_core(both)
    near = total(near_came, near[3], [both])
    near_came = scatter(near, 1)

    ahead, back, first, second, own = shares(
        gradient,
        partner,
        [(above, above_partner), (below, below_partner)],
        (1, 3),
        False,
        by_plane,
        [near[0]],
    )
    came = send(ahead, step(0, 1)), send(back, step(0, -1))
    (near,) = total(near_came, near[3], [ahead])

    other_half = send(near[Q:], lambda z, k, x, y: (z, 0, x, y) if k == 1 else None)
    far = hold(far, [near])
    far_partner = other_core(far)
    ahead, back, far_first, far_second, far_own = shares(
        gradient, partner, [(far, far_partner)], (2,), False, halved, [ahead]
    )
    far_came = send(ahead, step(0, 1)), send(back, step(0, -1))
    product, token = multiply(inv_root, [far, far_partner], [(2, 0), (2, 1)], product, F32, [ahead, other_half])
    came_again = second_step(came, first, second, far_came, far_first, far_second, [token])
    mirrored = [send(near[:Q], mirror(0))]
    product, token = multiply(
        inv_root, [above, above_partner], [(1, 0), (1, 1)], product, F32, [*came, *far_came, token]
    )
    rest = last_step(came, own, far_came, far_own, came_again, [token, mirrored[0]])
    (rest,) = total(scatter(rest, 1), rest[3])

    mirrored += [
        send(rest[Q : 2 * Q], mirror(3)),
        send(rest[2 * Q :], mirror(2)),
        send(rest[:Q], mirror(1)),
    ]
    out = messages(near, rest[: 2 * Q], rest[2 * Q :], mirrored, other_half)
    got = [out[0]] + [send(out[d], lambda z, k, x, y, d=d: (z, k, x + d, y)) for d in range(1, N)]
    product, token = multiply(inv_root, [below, below_partner], [(3, 0), (3, 1)], product, BF16, [out[0]])
    both, wanted = gathered(got, [token])
    return finish(both, other_core(wanted), stat_old), product


def solution(mesh):
    fine = Mesh(mesh.devices.reshape(N, 2, N, N), AXES)
    row, col = ("z", "core"), ("x", "y")
    return jax.shard_map(
        on_device,
        mesh=fine,
        in_specs=(P(row, col), P(row, col), P(row, None)),
        out_specs=(P(row, col), P(row, col)),
        check_vma=False,
    )
```

```python
import functools

import jax
import jax.numpy as jnp
from jax import lax
from jax.experimental import pallas as pl
from jax.experimental.pallas import tpu as pltpu
from jax.sharding import Mesh
from jax.sharding import PartitionSpec as P

N = 4
AXES = ("z", "core", "x", "y")
OFFSETS = (1, 3, 2, 0)
F32 = jnp.float32
BF16 = jnp.bfloat16
VMEM = pl.BlockSpec(memory_space=pltpu.VMEM)
ANY = pl.BlockSpec(memory_space=pl.ANY)


def shift(z, j):
    return jnp.where(j < z, 1, 0)


def first_row(z, j, q):
    return (q + shift(z, j)) & 3


def row_of(z, k, j, q):
    u = first_row(z, j, q)
    return (u + (k ^ (u >> 1))) & 3


def mirrored_row(z, k, j, q):
    u = first_row(z, j, q)
    return jnp.where(z == j, (q + 2 + k) & 3, (u + 3 - (k ^ (u >> 1))) & 3)


def linear(z, k, x, y):
    return (((z % N) * 2 + k) * N + x % N) * N + y % N


def devices():
    return [(z, k, x, y) for z in range(N) for k in range(2) for x in range(N) for y in range(N)]


def send(value, where):
    pairs = [(linear(*device), where(*device)) for device in devices()]
    return lax.ppermute(value, AXES, [(source, linear(*to)) for source, to in pairs if to is not None])


def up(n):
    return lambda z, k, x, y: (z + n, k, x, y)


def other_core(value):
    return send(value, lambda z, k, x, y: (z, 1 - k, x, y))


def coordinates():
    return tuple(lax.axis_index(name) for name in AXES)


def call(kernel, outs, operands, after=(), specs=None, scratch=(), vmem=24):
    n = len(operands)

    def body(*refs):
        kernel(*refs[:n], *refs[n + len(after) :])

    return pl.pallas_call(
        body,
        out_shape=outs,
        in_specs=list(specs or [VMEM] * n) + [ANY] * len(after),
        out_specs=[VMEM] * len(outs),
        scratch_shapes=list(scratch),
        compiler_params=pltpu.CompilerParams(vmem_limit_bytes=vmem * 2**20),
        cost_estimate=pl.CostEstimate(flops=1, bytes_accessed=1, transcendentals=0),
    )(*operands, *after)


def array(*shape, dtype=BF16):
    return jax.ShapeDtypeStruct(shape, dtype)


def shares(mine, theirs, others, turns, diagonal, places, after=()):
    rows, lat = mine.shape
    H = rows // 2
    Q = H // N
    tall = Q + (Q // 2 if diagonal else 0)

    def kernel(mine_ref, theirs_ref, *refs):
        out_refs = refs[2 * len(turns) :]
        z, k, x, y = coordinates()

        def rows_of(block, part, parts):
            start = pl.multiple_of((block & 1) * H + part * (H // parts), H // parts)
            window = pl.ds(start, H // parts)
            return jnp.where((block >> 1) == k, mine_ref[window, :], theirs_ref[window, :])

        def work(core):
            for t, turn in enumerate(turns):
                j = (z + turn) & 3
                for i, offset in enumerate(OFFSETS):
                    q = (y + offset) & 3
                    p = row_of(z, k, j, q)
                    window = pl.ds(pl.multiple_of((q & 1) * H, H), H)
                    right = jnp.where((q >> 1) == k, refs[2 * t][window, :], refs[2 * t + 1][window, :])
                    left = []
                    for offset in OFFSETS:
                        c = (x + offset) & 3
                        left.append(rows_of(p, c, N))
                        if diagonal:
                            left.append(rows_of((q + 2) & 3, k * N + c, 2 * N))
                    result = lax.dot_general(
                        jnp.concatenate(left, 0), right, (((1,), (1,)), ((), ())), preferred_element_type=F32
                    ).astype(BF16)
                    for m in range(N):
                        part, second = (m, i) if core == 0 else (i, m)
                        for out, to, start, size in places[part][t]:
                            rows_sent = slice(m * tall + start, m * tall + start + size)
                            out_refs[out][second, to : to + size, :] = result[rows_sent]

        for core in range(2):
            pl.when(k == core)(functools.partial(work, core))

    flat = [a for pair in others for a in pair]
    heights = {}
    for spots in places:
        for out, to, _, size in (piece for pieces in spots for piece in pieces):
            heights[out] = max(heights.get(out, 0), to + size)
    return call(kernel, [array(N, heights[out], H) for out in sorted(heights)], [mine, theirs, *flat], after)


def multiply(inv_root, tiles, blocks, start, dtype, after=()):
    rows, lat = tiles[0].shape
    height = inv_root.shape[0]
    step = height // N

    def kernel(root_ref, *refs):
        tile_refs, refs = refs[: len(tiles)], refs[len(tiles) :]
        out_ref, token_ref, held, sums, sems = refs[-5:]
        token_ref[...] = jnp.zeros_like(token_ref)
        z, k, _, _ = coordinates()

        def copy(i):
            turn, whose = blocks[i]
            block = 2 * ((z + turn) & 3) + (k if whose == 0 else 1 - k)
            columns = pl.ds(pl.multiple_of(block * rows, rows), rows)
            return pltpu.make_async_copy(root_ref.at[:, columns], held.at[i], sems.at[i])

        copy(0).start()
        for i, tile_ref in enumerate(tile_refs):
            if i + 1 < len(tiles):
                copy(i + 1).start()
            copy(i).wait()
            for r in range(N):
                part = slice(r * step, (r + 1) * step)
                term = jnp.dot(held[i, part, :], tile_ref[...], preferred_element_type=F32)
                if i > 0:
                    term = term + sums[part, :]
                elif start is not None:
                    term = term + refs[0][part, :]
                if i + 1 < len(tiles):
                    sums[part, :] = term
                else:
                    out_ref[part, :] = term.astype(dtype)

    more = [] if start is None else [start]
    return call(
        kernel,
        [array(height, lat, dtype=dtype), array(8, 128, dtype=F32)],
        [inv_root, *tiles, *more],
        after,
        vmem=42,
        specs=[ANY] + [VMEM] * (len(tiles) + len(more)),
        scratch=[pltpu.VMEM((len(tiles), height, rows), BF16), pltpu.VMEM((height, lat), F32), pltpu.SemaphoreType.DMA((len(tiles),))],
    )


def onward(above, below, after):
    def kernel(above_ref, below_ref, far_ref):
        k = lax.axis_index("core")
        far_ref[...] = jnp.where(k == 0, below_ref[...], above_ref[...])

    return call(kernel, [array(*above.shape)], [above, below], after)[0]


def together(above, below, after):
    def kernel(above_ref, below_ref, both_ref):
        both_ref[0] = above_ref[...]
        both_ref[1] = below_ref[...]

    return call(kernel, [array(2, *above.shape)], [above, below], after)[0]


def scatter(parts, stage):
    def where(z, k, x, y, n):
        return (z, k, x + n, y) if k == stage else (z, k, x, y + n)

    return [send(parts[r], functools.partial(where, n=OFFSETS[r])) for r in range(N - 1)]


def total(got, own, after=()):
    def kernel(*refs):
        value = refs[N - 1][...].astype(F32)
        for ref in refs[: N - 1]:
            value = value + ref[...].astype(F32)
        value = value.astype(BF16)
        for r, ref in enumerate(refs[N:]):
            ref[...] = value[r] if own.ndim == 3 else value

    outs = [array(*own.shape[1:])] * N if own.ndim == 3 else [array(*own.shape)]
    return call(kernel, outs, [*got, own], after)


def hold(value, after):
    def kernel(value_ref, out_ref):
        out_ref[...] = value_ref[...]

    return call(kernel, [array(*value.shape)], [value], after)[0]


def step(k, n):
    return lambda z, core, x, y: (z, core, x + n, y) if core == k else (z, core, x, y + n)


def second_step(came, first, second, far_came, far_first, far_second, after):
    Q, h = first.shape[1], far_first.shape[1]

    def kernel(ahead_ref, back_ref, first_ref, second_ref, ahead2_ref, back2_ref, first2_ref, second2_ref, to_ref, fro_ref):
        to_ref[:, :Q] = (first_ref[...].astype(F32) + ahead_ref[:, :Q].astype(F32)).astype(BF16)
        fro_ref[:, :Q] = (second_ref[...].astype(F32) + back_ref[:, Q:].astype(F32)).astype(BF16)
        to_ref[:, Q:] = (first2_ref[...].astype(F32) + ahead2_ref[:, :h].astype(F32)).astype(BF16)
        fro_ref[:, Q:] = (second2_ref[...].astype(F32) + back2_ref[:, h:].astype(F32)).astype(BF16)

    shape = array(first.shape[0], Q + h, first.shape[2])
    to, fro = call(kernel, [shape] * 2, [*came, first, second, *far_came, far_first, far_second], after)
    return send(to, step(0, 1)), send(fro, step(0, -1))


def last_step(came, own, far_came, far_own, came_again, after):
    Q = far_own.shape[1]
    h = Q // 2

    def kernel(ahead_ref, back_ref, own_ref, ahead2_ref, back2_ref, own2_ref, to_ref, fro_ref, *out_refs):
        def put(ref, at, *terms):
            value = terms[0].astype(F32)
            for term in terms[1:]:
                value = value + term.astype(F32)
            ref[at : at + terms[0].shape[0], :] = value.astype(BF16)

        for r, ref in enumerate(out_refs):
            put(ref, 0, own_ref[r, :Q], back_ref[r, :Q], to_ref[r, :Q])
            put(ref, Q, own_ref[r, Q:], ahead_ref[r, Q:], fro_ref[r, :Q])
            put(ref, 2 * Q, own2_ref[r, :h], back2_ref[r, :h], to_ref[r, Q:])
            put(ref, 2 * Q + h, own2_ref[r, h:], ahead2_ref[r, h:], fro_ref[r, Q:])

    outs = [array(3 * Q, own.shape[2])] * N
    return call(kernel, outs, [*came, own, *far_came, far_own, *came_again], after)


def mirror(turn):
    def where(z, k, x, y):
        j = (z + turn) % N
        u = (y + (j < z)) % N
        late = k ^ (u >> 1)
        p = (u + late) % N
        if turn == 0:
            return (z, 1, x, p) if late == 1 else None
        mirrored_u = (p + (z < j)) % N
        return (j, late ^ (mirrored_u >> 1), x, p)

    return where


def messages(near, middle, last, mirrored, other_half):
    Q = last.shape[0]
    H = last.shape[1]

    def kernel(near_ref, middle_ref, last_ref, m0_ref, m1_ref, m2_ref, m3_ref, half_ref, *out_refs):
        z, k, x, _ = coordinates()
        for d, out_ref in enumerate(out_refs):
            t = (x + d - z) & 3

            @pl.when(t == 0)
            def _(out_ref=out_ref):
                out_ref[:Q, :] = near_ref[:Q, :]
                out_ref[Q:, :] = jnp.where(k == 0, jnp.concatenate([near_ref[Q:, :], half_ref[...]], 0), m0_ref[...])

            for turn, (piece, mirrored_ref) in enumerate(
                ((middle_ref.at[:Q], m1_ref), (last_ref, m2_ref), (middle_ref.at[Q:], m3_ref)), 1
            ):

                @pl.when(t == turn)
                def _(out_ref=out_ref, piece=piece, mirrored_ref=mirrored_ref):
                    out_ref[:Q, :] = piece[...]
                    out_ref[Q:, :] = mirrored_ref[...]

    return call(kernel, [array(2 * Q, H)] * N, [near, middle, last, *mirrored, other_half])


def gathered(got, after):
    Q, H = got[0].shape[0] // 2, got[0].shape[1]

    def kernel(*refs):
        both_ref, wanted_ref = refs[N:]
        z, k, x, y = coordinates()
        for d in range(N):
            start = pl.multiple_of(((x - d) & 3) * Q, Q)
            for half in range(2):
                both_ref[half, pl.ds(start, Q), :] = refs[d][half * Q : (half + 1) * Q, :]
        stays = (row_of(z, k, x, y) >> 1) == k
        wanted_ref[...] = jnp.where(stays, both_ref[1], both_ref[0])

    return call(kernel, [array(2, H, H), array(H, H)], got, after)


def finish(both, arrived, stat_old):
    H = arrived.shape[0]
    E = H // 8

    def kernel(both_ref, arrived_ref, old_ref, out_ref):
        z, k, x, y = coordinates()

        def put(row, value):
            window = pl.ds(pl.multiple_of((row & 1) * H, H), H)
            out_ref[window, :] = 0.9 * old_ref[window, :] + 0.1 * value

        def turned(row, core, ref):
            whole = (z == x) & (core == 0)

            @pl.when(whole)
            def _():
                order = [2 * c + h for h in range(2) for c in range(N)]
                put(row, jnp.concatenate([ref[n * E : (n + 1) * E, :] for n in order], 0).astype(F32))

            @pl.when(jnp.logical_not(whole))
            def _():
                put(row, ref[...].astype(F32).T)

        plain, mirrored = row_of(z, k, x, y), mirrored_row(z, k, x, y)
        other_plain, other_mirrored = row_of(z, 1 - k, x, y), mirrored_row(z, 1 - k, x, y)

        @pl.when((plain >> 1) == k)
        def _():
            put(plain, both_ref[0].astype(F32))

        @pl.when((mirrored >> 1) == k)
        def _():
            turned(mirrored, k, both_ref.at[1])

        @pl.when((other_plain >> 1) == k)
        def _():
            put(other_plain, arrived_ref[...].astype(F32))

        @pl.when(((other_plain >> 1) != k) & ((other_mirrored >> 1) == k))
        def _():
            turned(other_mirrored, 1 - k, arrived_ref)

    return call(kernel, [array(2 * H, H, dtype=F32)], [both, arrived, stat_old])[0]


def on_device(gradient, stat_old, inv_root):
    Q = gradient.shape[0] // 8

    above = send(gradient, up(-1))
    below = send(gradient, up(1))
    partner = other_core(gradient)

    tall = Q + Q // 2
    straight = [[[(r, 0, 0, tall)]] for r in range(N)]
    h = Q // 2
    halved = [
        [[(2, 0, 0, h), (0, h, h, h)]],
        [[(1, 0, 0, h), (3, 0, h, h)]],
        [[(0, 0, 0, h), (1, h, h, h)]],
        [[(4, 0, 0, Q)]],
    ]
    by_plane = [
        [[(2, 0, 0, Q)], [(0, Q, 0, Q)]],
        [[(1, 0, 0, Q)], [(3, 0, 0, Q)]],
        [[(0, 0, 0, Q)], [(1, Q, 0, Q)]],
        [[(4, 0, 0, Q)], [(4, Q, 0, Q)]],
    ]
    near = shares(gradient, partner, [(gradient, partner)], (0,), True, straight)
    near_came = scatter(near, 0)
    product, token = multiply(inv_root, [gradient, partner], [(0, 0), (0, 1)], None, F32, [near[0]])

    passed = onward(above, below, [token])
    both = together(above, below, [passed, *near_came])
    far = send(passed, lambda z, k, x, y: (z + 1 - 2 * k, k, x, y))
    above_partner, below_partner = other_core(both)
    near = total(near_came, near[3], [both])
    near_came = scatter(near, 1)

    ahead, back, first, second, own = shares(
        gradient,
        partner,
        [(above, above_partner), (below, below_partner)],
        (1, 3),
        False,
        by_plane,
        [near[0]],
    )
    came = send(ahead, step(0, 1)), send(back, step(0, -1))
    (near,) = total(near_came, near[3], [ahead])

    other_half = send(near[Q:], lambda z, k, x, y: (z, 0, x, y) if k == 1 else None)
    far = hold(far, [near])
    far_partner = other_core(far)
    ahead, back, far_first, far_second, far_own = shares(
        gradient, partner, [(far, far_partner)], (2,), False, halved, [ahead]
    )
    far_came = send(ahead, step(0, 1)), send(back, step(0, -1))
    product, token = multiply(inv_root, [far, far_partner], [(2, 0), (2, 1)], product, F32, [ahead, other_half])
    came_again = second_step(came, first, second, far_came, far_first, far_second, [token])
    mirrored = [send(near[:Q], mirror(0))]
    product, token = multiply(
        inv_root, [above, above_partner], [(1, 0), (1, 1)], product, F32, [*came, *far_came, token]
    )
    rest = last_step(came, own, far_came, far_own, came_again, [token, mirrored[0]])
    (rest,) = total(scatter(rest, 1), rest[3])

    mirrored += [
        send(rest[Q : 2 * Q], mirror(3)),
        send(rest[2 * Q :], mirror(2)),
        send(rest[:Q], mirror(1)),
    ]
    out = messages(near, rest[: 2 * Q], rest[2 * Q :], mirrored, other_half)
    got = [out[0]] + [send(out[d], lambda z, k, x, y, d=d: (z, k, x + d, y)) for d in range(1, N)]
    product, token = multiply(inv_root, [below, below_partner], [(3, 0), (3, 1)], product, BF16, [out[0]])
    both, wanted = gathered(got, [token])
    return finish(both, other_core(wanted), stat_old), product


def solution(mesh):
    fine = Mesh(mesh.devices.reshape(N, 2, N, N), AXES)
    row, col = ("z", "core"), ("x", "y")
    return jax.shard_map(
        on_device,
        mesh=fine,
        in_specs=(P(row, col), P(row, col), P(row, None)),
        out_specs=(P(row, col), P(row, col)),
        check_vma=False,
    )
```

```python
import functools

import jax
import jax.numpy as jnp
from jax import lax
from jax.experimental import pallas as pl
from jax.experimental.pallas import tpu as pltpu
from jax.sharding import Mesh
from jax.sharding import PartitionSpec as P

N = 4
AXES = ("z", "core", "x", "y")
OFFSETS = (1, 3, 2, 0)
F32 = jnp.float32
BF16 = jnp.bfloat16
VMEM = pl.BlockSpec(memory_space=pltpu.VMEM)
ANY = pl.BlockSpec(memory_space=pl.ANY)


def shift(z, j):
    return jnp.where(j < z, 1, 0)


def first_row(z, j, q):
    return (q + shift(z, j)) & 3


def row_of(z, k, j, q):
    u = first_row(z, j, q)
    return (u + (k ^ (u >> 1))) & 3


def mirrored_row(z, k, j, q):
    u = first_row(z, j, q)
    return jnp.where(z == j, (q + 2 + k) & 3, (u + 3 - (k ^ (u >> 1))) & 3)


def linear(z, k, x, y):
    return (((z % N) * 2 + k) * N + x % N) * N + y % N


def devices():
    return [(z, k, x, y) for z in range(N) for k in range(2) for x in range(N) for y in range(N)]


def send(value, where):
    pairs = [(linear(*device), where(*device)) for device in devices()]
    return lax.ppermute(value, AXES, [(source, linear(*to)) for source, to in pairs if to is not None])


def up(n):
    return lambda z, k, x, y: (z + n, k, x, y)


def other_core(value):
    return send(value, lambda z, k, x, y: (z, 1 - k, x, y))


def coordinates():
    return tuple(lax.axis_index(name) for name in AXES)


def call(kernel, outs, operands, after=(), specs=None, scratch=(), vmem=24):
    n = len(operands)

    def body(*refs):
        kernel(*refs[:n], *refs[n + len(after) :])

    return pl.pallas_call(
        body,
        out_shape=outs,
        in_specs=list(specs or [VMEM] * n) + [ANY] * len(after),
        out_specs=[VMEM] * len(outs),
        scratch_shapes=list(scratch),
        compiler_params=pltpu.CompilerParams(vmem_limit_bytes=vmem * 2**20),
        cost_estimate=pl.CostEstimate(flops=1, bytes_accessed=1, transcendentals=0),
    )(*operands, *after)


def array(*shape, dtype=BF16):
    return jax.ShapeDtypeStruct(shape, dtype)


def shares(mine, theirs, others, turns, diagonal, places, after=()):
    rows, lat = mine.shape
    H = rows // 2
    Q = H // N
    tall = Q + (Q // 2 if diagonal else 0)

    def kernel(mine_ref, theirs_ref, *refs):
        out_refs = refs[2 * len(turns) :]
        z, k, x, y = coordinates()

        def rows_of(block, part, parts):
            start = pl.multiple_of((block & 1) * H + part * (H // parts), H // parts)
            window = pl.ds(start, H // parts)
            return jnp.where((block >> 1) == k, mine_ref[window, :], theirs_ref[window, :])

        def work(core):
            for t, turn in enumerate(turns):
                j = (z + turn) & 3
                for i, offset in enumerate(OFFSETS):
                    q = (y + offset) & 3
                    p = row_of(z, k, j, q)
                    window = pl.ds(pl.multiple_of((q & 1) * H, H), H)
                    right = jnp.where((q >> 1) == k, refs[2 * t][window, :], refs[2 * t + 1][window, :])
                    left = []
                    for offset in OFFSETS:
                        c = (x + offset) & 3
                        left.append(rows_of(p, c, N))
                        if diagonal:
                            left.append(rows_of((q + 2) & 3, k * N + c, 2 * N))
                    result = lax.dot_general(
                        jnp.concatenate(left, 0), right, (((1,), (1,)), ((), ())), preferred_element_type=F32
                    ).astype(BF16)
                    for m in range(N):
                        part, second = (m, i) if core == 0 else (i, m)
                        for out, to, start, size in places[part][t]:
                            rows_sent = slice(m * tall + start, m * tall + start + size)
                            out_refs[out][second, to : to + size, :] = result[rows_sent]

        for core in range(2):
            pl.when(k == core)(functools.partial(work, core))

    flat = [a for pair in others for a in pair]
    heights = {}
    for spots in places:
        for out, to, _, size in (piece for pieces in spots for piece in pieces):
            heights[out] = max(heights.get(out, 0), to + size)
    return call(kernel, [array(N, heights[out], H) for out in sorted(heights)], [mine, theirs, *flat], after)


def multiply(inv_root, tiles, blocks, start, dtype, after=()):
    rows, lat = tiles[0].shape
    height = inv_root.shape[0]
    step = height // N

    def kernel(root_ref, *refs):
        tile_refs, refs = refs[: len(tiles)], refs[len(tiles) :]
        out_ref, token_ref, held, sums, sems = refs[-5:]
        token_ref[...] = jnp.zeros_like(token_ref)
        z, k, _, _ = coordinates()

        def copy(i):
            turn, whose = blocks[i]
            block = 2 * ((z + turn) & 3) + (k if whose == 0 else 1 - k)
            columns = pl.ds(pl.multiple_of(block * rows, rows), rows)
            return pltpu.make_async_copy(root_ref.at[:, columns], held.at[i], sems.at[i])

        copy(0).start()
        for i, tile_ref in enumerate(tile_refs):
            if i + 1 < len(tiles):
                copy(i + 1).start()
            copy(i).wait()
            for r in range(N):
                part = slice(r * step, (r + 1) * step)
                term = jnp.dot(held[i, part, :], tile_ref[...], preferred_element_type=F32)
                if i > 0:
                    term = term + sums[part, :]
                elif start is not None:
                    term = term + refs[0][part, :]
                if i + 1 < len(tiles):
                    sums[part, :] = term
                else:
                    out_ref[part, :] = term.astype(dtype)

    more = [] if start is None else [start]
    return call(
        kernel,
        [array(height, lat, dtype=dtype), array(8, 128, dtype=F32)],
        [inv_root, *tiles, *more],
        after,
        vmem=42,
        specs=[ANY] + [VMEM] * (len(tiles) + len(more)),
        scratch=[pltpu.VMEM((len(tiles), height, rows), BF16), pltpu.VMEM((height, lat), F32), pltpu.SemaphoreType.DMA((len(tiles),))],
    )


def onward(above, below, after):
    def kernel(above_ref, below_ref, far_ref):
        k = lax.axis_index("core")
        far_ref[...] = jnp.where(k == 0, below_ref[...], above_ref[...])

    return call(kernel, [array(*above.shape)], [above, below], after)[0]


def together(above, below, after):
    def kernel(above_ref, below_ref, both_ref):
        both_ref[0] = above_ref[...]
        both_ref[1] = below_ref[...]

    return call(kernel, [array(2, *above.shape)], [above, below], after)[0]


def scatter(parts, stage):
    def where(z, k, x, y, n):
        return (z, k, x + n, y) if k == stage else (z, k, x, y + n)

    came = {r: send(parts[r], functools.partial(where, n=OFFSETS[r])) for r in (2, 0, 1)}
    return [came[r] for r in range(N - 1)]


def total(got, own, after=()):
    def kernel(*refs):
        value = refs[N - 1][...].astype(F32)
        for ref in refs[: N - 1]:
            value = value + ref[...].astype(F32)
        value = value.astype(BF16)
        for r, ref in enumerate(refs[N:]):
            ref[...] = value[r] if own.ndim == 3 else value

    outs = [array(*own.shape[1:])] * N if own.ndim == 3 else [array(*own.shape)]
    return call(kernel, outs, [*got, own], after)


def hold(value, after):
    def kernel(value_ref, out_ref):
        out_ref[...] = value_ref[...]

    return call(kernel, [array(*value.shape)], [value], after)[0]


def step(k, n):
    return lambda z, core, x, y: (z, core, x + n, y) if core == k else (z, core, x, y + n)


def second_step(came, first, second, far_came, far_first, far_second, after):
    Q, h = first.shape[1], far_first.shape[1]

    def kernel(ahead_ref, back_ref, first_ref, second_ref, ahead2_ref, back2_ref, first2_ref, second2_ref, to_ref, fro_ref):
        to_ref[:, :Q] = (first_ref[...].astype(F32) + ahead_ref[:, :Q].astype(F32)).astype(BF16)
        fro_ref[:, :Q] = (second_ref[...].astype(F32) + back_ref[:, Q:].astype(F32)).astype(BF16)
        to_ref[:, Q:] = (first2_ref[...].astype(F32) + ahead2_ref[:, :h].astype(F32)).astype(BF16)
        fro_ref[:, Q:] = (second2_ref[...].astype(F32) + back2_ref[:, h:].astype(F32)).astype(BF16)

    shape = array(first.shape[0], Q + h, first.shape[2])
    to, fro = call(kernel, [shape] * 2, [*came, first, second, *far_came, far_first, far_second], after)
    return send(to, step(0, 1)), send(fro, step(0, -1))


def last_step(came, own, far_came, far_own, came_again, after):
    Q = far_own.shape[1]
    h = Q // 2

    def kernel(ahead_ref, back_ref, own_ref, ahead2_ref, back2_ref, own2_ref, to_ref, fro_ref, *out_refs):
        def put(ref, at, *terms):
            value = terms[0].astype(F32)
            for term in terms[1:]:
                value = value + term.astype(F32)
            ref[at : at + terms[0].shape[0], :] = value.astype(BF16)

        for r, ref in enumerate(out_refs):
            put(ref, 0, own_ref[r, :Q], back_ref[r, :Q], to_ref[r, :Q])
            put(ref, Q, own_ref[r, Q:], ahead_ref[r, Q:], fro_ref[r, :Q])
            put(ref, 2 * Q, own2_ref[r, :h], back2_ref[r, :h], to_ref[r, Q:])
            put(ref, 2 * Q + h, own2_ref[r, h:], ahead2_ref[r, h:], fro_ref[r, Q:])

    outs = [array(3 * Q, own.shape[2])] * N
    return call(kernel, outs, [*came, own, *far_came, far_own, *came_again], after)


def mirror(turn):
    def where(z, k, x, y):
        j = (z + turn) % N
        u = (y + (j < z)) % N
        late = k ^ (u >> 1)
        p = (u + late) % N
        if turn == 0:
            return (z, 1, x, p) if late == 1 else None
        mirrored_u = (p + (z < j)) % N
        return (j, late ^ (mirrored_u >> 1), x, p)

    return where


def messages(near, middle, last, mirrored, other_half):
    Q = last.shape[0]
    H = last.shape[1]

    def kernel(near_ref, middle_ref, last_ref, m0_ref, m1_ref, m2_ref, m3_ref, half_ref, *out_refs):
        z, k, x, _ = coordinates()
        for d, out_ref in enumerate(out_refs):
            t = (x + d - z) & 3

            @pl.when(t == 0)
            def _(out_ref=out_ref):
                out_ref[:Q, :] = near_ref[:Q, :]
                out_ref[Q:, :] = jnp.where(k == 0, jnp.concatenate([near_ref[Q:, :], half_ref[...]], 0), m0_ref[...])

            for turn, (piece, mirrored_ref) in enumerate(
                ((middle_ref.at[:Q], m1_ref), (last_ref, m2_ref), (middle_ref.at[Q:], m3_ref)), 1
            ):

                @pl.when(t == turn)
                def _(out_ref=out_ref, piece=piece, mirrored_ref=mirrored_ref):
                    out_ref[:Q, :] = piece[...]
                    out_ref[Q:, :] = mirrored_ref[...]

    return call(kernel, [array(2 * Q, H)] * N, [near, middle, last, *mirrored, other_half])


def gathered(got, after):
    Q, H = got[0].shape[0] // 2, got[0].shape[1]

    def kernel(*refs):
        both_ref, wanted_ref = refs[N:]
        z, k, x, y = coordinates()
        for d in range(N):
            start = pl.multiple_of(((x - d) & 3) * Q, Q)
            for half in range(2):
                both_ref[half, pl.ds(start, Q), :] = refs[d][half * Q : (half + 1) * Q, :]
        stays = (row_of(z, k, x, y) >> 1) == k
        wanted_ref[...] = jnp.where(stays, both_ref[1], both_ref[0])

    return call(kernel, [array(2, H, H), array(H, H)], got, after)


def finish(both, arrived, stat_old):
    H = arrived.shape[0]
    E = H // 8

    def kernel(both_ref, arrived_ref, old_ref, out_ref):
        z, k, x, y = coordinates()

        def put(row, value):
            window = pl.ds(pl.multiple_of((row & 1) * H, H), H)
            out_ref[window, :] = 0.9 * old_ref[window, :] + 0.1 * value

        def turned(row, core, ref):
            whole = (z == x) & (core == 0)

            @pl.when(whole)
            def _():
                order = [2 * c + h for h in range(2) for c in range(N)]
                put(row, jnp.concatenate([ref[n * E : (n + 1) * E, :] for n in order], 0).astype(F32))

            @pl.when(jnp.logical_not(whole))
            def _():
                put(row, ref[...].astype(F32).T)

        plain, mirrored = row_of(z, k, x, y), mirrored_row(z, k, x, y)
        other_plain, other_mirrored = row_of(z, 1 - k, x, y), mirrored_row(z, 1 - k, x, y)

        @pl.when((plain >> 1) == k)
        def _():
            put(plain, both_ref[0].astype(F32))

        @pl.when((mirrored >> 1) == k)
        def _():
            turned(mirrored, k, both_ref.at[1])

        @pl.when((other_plain >> 1) == k)
        def _():
            put(other_plain, arrived_ref[...].astype(F32))

        @pl.when(((other_plain >> 1) != k) & ((other_mirrored >> 1) == k))
        def _():
            turned(other_mirrored, 1 - k, arrived_ref)

    return call(kernel, [array(2 * H, H, dtype=F32)], [both, arrived, stat_old])[0]


def on_device(gradient, stat_old, inv_root):
    Q = gradient.shape[0] // 8

    above = send(gradient, up(-1))
    below = send(gradient, up(1))
    partner = other_core(gradient)

    tall = Q + Q // 2
    straight = [[[(r, 0, 0, tall)]] for r in range(N)]
    h = Q // 2
    halved = [
        [[(2, 0, 0, h), (0, h, h, h)]],
        [[(1, 0, 0, h), (3, 0, h, h)]],
        [[(0, 0, 0, h), (1, h, h, h)]],
        [[(4, 0, 0, Q)]],
    ]
    by_plane = [
        [[(2, 0, 0, Q)], [(0, Q, 0, Q)]],
        [[(1, 0, 0, Q)], [(3, 0, 0, Q)]],
        [[(0, 0, 0, Q)], [(1, Q, 0, Q)]],
        [[(4, 0, 0, Q)], [(4, Q, 0, Q)]],
    ]
    near = shares(gradient, partner, [(gradient, partner)], (0,), True, straight)
    near_came = scatter(near, 0)
    product, token = multiply(inv_root, [gradient, partner], [(0, 0), (0, 1)], None, F32, [near[0]])

    passed = onward(above, below, [token])
    both = together(above, below, [passed, *near_came])
    far = send(passed, lambda z, k, x, y: (z + 1 - 2 * k, k, x, y))
    above_partner, below_partner = other_core(both)
    near = total(near_came, near[3], [both])
    near_came = scatter(near, 1)

    ahead, back, first, second, own = shares(
        gradient,
        partner,
        [(above, above_partner), (below, below_partner)],
        (1, 3),
        False,
        by_plane,
        [near[0]],
    )
    came = send(ahead, step(0, 1)), send(back, step(0, -1))
    (near,) = total(near_came, near[3], [ahead])

    other_half = send(near[Q:], lambda z, k, x, y: (z, 0, x, y) if k == 1 else None)
    far = hold(far, [near])
    far_partner = other_core(far)
    ahead, back, far_first, far_second, far_own = shares(
        gradient, partner, [(far, far_partner)], (2,), False, halved, [ahead]
    )
    far_came = send(ahead, step(0, 1)), send(back, step(0, -1))
    product, token = multiply(inv_root, [far, far_partner], [(2, 0), (2, 1)], product, F32, [ahead, other_half])
    came_again = second_step(came, first, second, far_came, far_first, far_second, [token])
    mirrored = [send(near[:Q], mirror(0))]
    product, token = multiply(
        inv_root, [above, above_partner], [(1, 0), (1, 1)], product, F32, [*came, *far_came, token]
    )
    rest = last_step(came, own, far_came, far_own, came_again, [token, mirrored[0]])
    (rest,) = total(scatter(rest, 1), rest[3])

    from_far = send(rest[2 * Q :], mirror(2))
    mirrored += [send(rest[Q : 2 * Q], mirror(3)), from_far, send(rest[:Q], mirror(1))]
    out = messages(near, rest[: 2 * Q], rest[2 * Q :], mirrored, other_half)
    came = {d: send(out[d], lambda z, k, x, y, d=d: (z, k, x + d, y)) for d in (2, 1, 3)}
    got = [out[0]] + [came[d] for d in range(1, N)]
    product, token = multiply(inv_root, [below, below_partner], [(3, 0), (3, 1)], product, BF16, [out[0]])
    both, wanted = gathered(got, [token])
    return finish(both, other_core(wanted), stat_old), product


def solution(mesh):
    fine = Mesh(mesh.devices.reshape(N, 2, N, N), AXES)
    row, col = ("z", "core"), ("x", "y")
    return jax.shard_map(
        on_device,
        mesh=fine,
        in_specs=(P(row, col), P(row, col), P(row, None)),
        out_specs=(P(row, col), P(row, col)),
        check_vma=False,
    )
```
